128 devices in a mesh: brick: 16 (over y, x), sub: 8 (over z, core).
Axes of the slice: x: 4, y: 4, z: 4, core: 2. Of those that a mesh axis runs over, the one named last changes fastest.
Arguments:
- field_start: float32 [8192, 16, 256], P(('brick', 'sub')), may hold values from -6 to 6
- source: float32 [8192, 16, 256], P(('brick', 'sub')), may hold values from -24 to 24
- diffusion: float32 [8192, 16, 256], P(('brick', 'sub')), may hold values from 0.2 to 5
- decay_rate: float32 [8192, 16, 256], P(('brick', 'sub')), may hold values from 0.5 to 8
- neighbour: int32 [8192, 6], P(('brick', 'sub')), may hold values from -1 to 49151, as said below
- coarse_source: int32 [1024], P(('brick', 'sub')), may hold values from 0 to 1023, as said below
Outputs:
- smoothed: float32 [8192, 16, 256], P(('brick', 'sub'))
- moved_coarse: float32 [1024, 3, 16, 256], P(('brick', 'sub'))
The draws below stay inside these ranges and needn't reach their ends.
Inputs may be any that keep to these rules, and one draw needn't show every extreme that they name: `neighbour`: bricks are numbered 64 per device in the order of the joined axis brick+sub. A brick borders only bricks of its own device or of the devices one step away along brick or along sub. Face f of a brick borders face f xor 1 of another brick or nothing (-1), and the relation is symmetric. At most 16 faces of one device border the device one step along brick, and at most 16 the device one step along sub; some pairs of devices reach each. `coarse_source`: A permutation of the level-2 bricks. A level-2 brick moves only between devices of the same index along sub. Each device receives 1 of its slots' bricks from each of 8 devices (possibly itself) and hands 1 of its own to each of 8.
All inputs are finite; a program needn't handle non-finite values.
Results may differ from the reference program's by a relative error of at most 0.00007.
Values sent between devices are 32-bit elements; how exact they have to be, the bound alone decides.
No kernel may reach another device: no remote copies, remote signals or barrier semaphores. Data moves between devices by JAX's collectives and lax.ppermute only.
A program may use at most 128 MiB of HBM per device.

```python
import math
import jax
import jax.numpy as jnp

BRICK_EDGE = 16
EDGE = 4
LZ = 4
SWEEPS = 2
BRK_DEV = 64
BRICKS = 8192
COARSE_DEV = 8
COARSE = 1024
MOVE_CAP = 1
N_BRICK = 16
N_SUB = 8


def distinct_order(key, rows_total, width):
    scores = jax.random.randint(key, (rows_total, width), 0, 1 << 20) * width + jnp.arange(width, dtype=jnp.int32)[None, :]
    return jnp.argsort(scores, axis=1).astype(jnp.int32)


def draw_neighbour(key, part):
    key = jax.random.fold_in(key, 11)
    device_total = N_BRICK * N_SUB
    extents = [N_BRICK, 1, N_SUB]
    block_sides = [EDGE, EDGE, LZ]
    brick_ids = jnp.arange(BRICKS, dtype=jnp.int32)
    device_ids = brick_ids // BRK_DEV
    local_ids = brick_ids % BRK_DEV
    local_coords = [local_ids % EDGE, local_ids // EDGE % EDGE, local_ids // (EDGE * EDGE)]
    device_coords = [device_ids // N_SUB, jnp.zeros_like(device_ids), device_ids % N_SUB]
    global_coords = [device_coords[axis_number] * block_sides[axis_number] + local_coords[axis_number] for axis_number in range(3)]
    cut_key, spared_key = jax.random.split(key)
    severed_bits = jax.random.randint(cut_key, (BRICKS, 3), 0, 4) == 0
    spared_device = jax.random.randint(spared_key, (), 0, device_total)
    columns = []
    for face_number in range(6):
        axis_number = face_number // 2
        direction = 2 * (face_number % 2) - 1
        limit = extents[axis_number] * block_sides[axis_number]
        shifted = list(global_coords)
        shifted[axis_number] = global_coords[axis_number] + direction
        inside = (shifted[axis_number] >= 0) & (shifted[axis_number] < limit)
        clipped = [jnp.clip(shifted[other_axis], 0, extents[other_axis] * block_sides[other_axis] - 1) for other_axis in range(3)]
        other_device = clipped[0] // EDGE * N_SUB + clipped[2] // LZ
        other_local = (clipped[2] % LZ * EDGE + clipped[1] % EDGE) * EDGE + clipped[0] % EDGE
        other_brick = other_device * BRK_DEV + other_local
        lower_brick = other_brick if direction < 0 else brick_ids
        severed = severed_bits[lower_brick, axis_number] & (device_ids != spared_device) & (other_device != spared_device)
        columns.append(jnp.where(inside & jnp.logical_not(severed), other_brick * 6 + (face_number ^ 1), -1))
    return jnp.stack(columns, axis=1).astype(jnp.int32)


def draw_coarse_source(key, part):
    key = jax.random.fold_in(key, 23)
    device_total = N_BRICK * N_SUB
    subkeys = jax.random.split(key, 4)
    shuffle = distinct_order(subkeys[0], N_SUB, N_BRICK)
    inverse = jnp.argsort(shuffle, axis=1).astype(jnp.int32)
    offsets = distinct_order(subkeys[1], 1, N_BRICK)[0, :8]
    sender_order = distinct_order(subkeys[2], device_total, COARSE_DEV)
    slot_order = distinct_order(subkeys[3], device_total, COARSE_DEV)
    senders = jnp.arange(device_total, dtype=jnp.int32)[:, None]
    sender_row = senders // N_SUB
    sender_sub = senders % N_SUB
    places = jnp.arange(COARSE_DEV, dtype=jnp.int32)[None, :]
    groups = places // MOVE_CAP
    target_row = shuffle[sender_sub, (inverse[sender_sub, sender_row] + offsets[groups]) % N_BRICK]
    targets = target_row * N_SUB + sender_sub
    slots = slot_order[targets, jnp.broadcast_to(places, targets.shape)]
    sources = senders * COARSE_DEV + sender_order
    return jnp.zeros((COARSE,), jnp.int32).at[(targets * COARSE_DEV + slots).reshape(-1)].set(sources.reshape(-1))


def steps_of(own_key, shape, cuts, smallest, top_value):
    gain, own = 1.0, jax.random.fold_in(own_key, 6)
    for dim, blocks in cuts:
        draws = jnp.exp(jax.random.uniform(jax.random.fold_in(own, dim), (blocks,), jnp.float32, smallest / len(cuts), top_value / len(cuts)))
        gain = gain * jnp.repeat(draws, shape[dim] // blocks).reshape([-1 if axis == dim else 1 for axis in range(len(shape))])
    return gain


def centred(rng, shape, scale, reach, cuts=(), held_as=jnp.bfloat16):
    values = jax.random.normal(rng, shape, jnp.float32) * scale
    if len(cuts) > 0:
        values = steps_of(rng, shape, cuts, -0.22, 0.18) * values
    return jnp.clip(values, min=-reach, max=reach).astype(held_as)


def setup_inputs(seed: int = 0) -> dict:
    splits = jax.random.split(jax.random.key(seed), 7)
    field_start = centred(splits[0], (BRICKS, BRICK_EDGE, BRICK_EDGE * BRICK_EDGE), 1.0, 6.0, ((0, 128),), jnp.float32)
    source = centred(splits[1], (BRICKS, BRICK_EDGE, BRICK_EDGE * BRICK_EDGE), 4.0, 24.0, ((0, 128),), jnp.float32)
    diffusion = jnp.clip(jnp.exp(math.log(5.0) - 3.218876 * jax.random.uniform(splits[2], (BRICKS, BRICK_EDGE, BRICK_EDGE * BRICK_EDGE), jnp.float32) ** steps_of(splits[2], (BRICKS, BRICK_EDGE, BRICK_EDGE * BRICK_EDGE), ((0, 128),), -0.2, 0.2)), 0.2, 5.0)
    decay_rate = jnp.clip(jnp.exp(math.log(8.0) - 2.7725887 * jax.random.uniform(splits[3], (BRICKS, BRICK_EDGE, BRICK_EDGE * BRICK_EDGE), jnp.float32) ** steps_of(splits[3], (BRICKS, BRICK_EDGE, BRICK_EDGE * BRICK_EDGE), ((0, 128),), -0.2, 0.2)), 0.5, 8.0)
    neighbour = draw_neighbour(jax.random.fold_in(splits[6], 71), 0)
    coarse_source = draw_coarse_source(jax.random.fold_in(splits[6], 71), 0)
    return {"field_start": field_start, "source": source, "diffusion": diffusion, "decay_rate": decay_rate, "neighbour": neighbour, "coarse_source": coarse_source}


OMEGA = 0.8


def faces_of(grid_field):
    bricks_here, brick_edge, plane_size = grid_field.shape
    cube = grid_field.reshape(bricks_here, brick_edge, brick_edge, brick_edge)
    planes = [cube[:, :, :, 0], cube[:, :, :, brick_edge - 1], cube[:, :, 0, :], cube[:, :, brick_edge - 1, :], cube[:, 0, :, :], cube[:, brick_edge - 1, :, :]]
    return jnp.stack([plane_cut.reshape(bricks_here, plane_size) for plane_cut in planes], axis=1)


def beside(grid_field, ghosts):
    bricks_here, brick_edge, plane_size = grid_field.shape
    column = jnp.arange(plane_size) % brick_edge

    def spread(ghost_face):
        return jnp.repeat(ghost_face.reshape(bricks_here, brick_edge, brick_edge), brick_edge, axis=2)

    zero_column = jnp.zeros((bricks_here, brick_edge, 1), grid_field.dtype)
    x_lower = jnp.where(column == 0, spread(ghosts[:, 0]), jnp.concatenate([zero_column, grid_field[:, :, :-1]], axis=2))
    x_upper = jnp.where(column == brick_edge - 1, spread(ghosts[:, 1]), jnp.concatenate([grid_field[:, :, 1:], zero_column], axis=2))
    y_lower = jnp.concatenate([ghosts[:, 2].reshape(bricks_here, brick_edge, brick_edge), grid_field[:, :, :-brick_edge]], axis=2)
    y_upper = jnp.concatenate([grid_field[:, :, brick_edge:], ghosts[:, 3].reshape(bricks_here, brick_edge, brick_edge)], axis=2)
    z_lower = jnp.concatenate([ghosts[:, 4][:, None, :], grid_field[:, :-1, :]], axis=1)
    z_upper = jnp.concatenate([grid_field[:, 1:, :], ghosts[:, 5][:, None, :]], axis=1)
    return [x_lower, x_upper, y_lower, y_upper, z_lower, z_upper]


def coefficients(diffusion, decay_rate, kappa_ghosts):
    link_fields = [0.5 * (diffusion + neighbour_value) for neighbour_value in beside(diffusion, kappa_ghosts)]
    diagonal = decay_rate
    for link_field in link_fields:
        diagonal = diagonal + link_field
    return link_fields, diagonal


def apply_operator(grid_field, ghosts, link_fields, decay_rate):
    applied = decay_rate * grid_field
    for link_field, neighbour_value in zip(link_fields, beside(grid_field, ghosts)):
        applied = applied + link_field * (grid_field - neighbour_value)
    return applied


def restrict(residual):
    bricks_here, brick_edge, plane_size = residual.shape
    half_edge = brick_edge // 2
    devices_here = bricks_here // BRK_DEV
    fine_cells = residual.reshape(devices_here, LZ, EDGE, EDGE, half_edge, 2, half_edge, 2, half_edge, 2)
    averaged = jnp.sum(fine_cells, axis=(5, 7, 9)) * 0.125
    grouped = averaged.reshape(devices_here, LZ // 2, 2, EDGE // 2, 2, EDGE // 2, 2, half_edge, half_edge, half_edge)
    grouped = jnp.transpose(grouped, (0, 1, 3, 5, 2, 7, 4, 8, 6, 9))
    return grouped.reshape(devices_here * (LZ // 2) * (EDGE // 2) * (EDGE // 2), brick_edge, plane_size)


def reference(field_start, source, diffusion, decay_rate, neighbour, coarse_source):
    bricks_total, brick_edge, plane_size = field_start.shape
    face_total = bricks_total * 6
    links_face = neighbour.reshape(-1).astype(jnp.int32)
    table_rows = jnp.where(links_face < 0, face_total, links_face).astype(jnp.int32)

    def ghosts_of(grid_field):
        face_table = faces_of(grid_field).reshape(face_total, plane_size)
        face_table = jnp.concatenate([face_table, jnp.zeros((1, plane_size), face_table.dtype)], axis=0)
        return jnp.take(face_table, table_rows, axis=0).reshape(bricks_total, 6, plane_size)

    link_fields, diagonal = coefficients(diffusion, decay_rate, ghosts_of(diffusion))
    field_now = field_start
    for sweep_number in range(SWEEPS):
        applied = apply_operator(field_now, ghosts_of(field_now), link_fields, decay_rate)
        field_now = field_now + OMEGA * (source - applied) / diagonal
    residual = source - apply_operator(field_now, ghosts_of(field_now), link_fields, decay_rate)
    coarse = jnp.stack([restrict(residual), restrict(diffusion), restrict(decay_rate)], axis=1)
    moved_coarse = jnp.take(coarse, coarse_source.astype(jnp.int32), axis=0)
    return field_now, moved_coarse
```

```python
import functools

import jax
import jax.numpy as jnp
from jax import lax
from jax.experimental import pallas as pl
from jax.experimental.pallas import tpu as pltpu
from jax.sharding import PartitionSpec as P

EDGE = 4
LZ = 4
SWEEPS = 2
OMEGA = 0.8

SIDE = 16
PLANE = SIDE * SIDE
HALF = PLANE // 2
BRK = EDGE * EDGE * LZ
FACES = 6 * BRK
COARSE_DEV = BRK // 8
CAP = 16
PEERS = 4
ZERO_BRICK = BRK
MESSAGE_BRICK = BRK + 1
SLOT_BRICK = MESSAGE_BRICK + PEERS
EXT_BRICKS = SLOT_BRICK + PEERS * CAP
SEND_ROW = 6
ODD_ROW = 7
F32 = jnp.float32
I32 = jnp.int32
VMEM_LIMIT = 40 * 1024 * 1024


def native_place(face):
    return SIDE - 1 if face % 2 == 0 else 0


def lane_iota(shape):
    return lax.broadcasted_iota(I32, shape, len(shape) - 1)


def row_iota(shape):
    return lax.broadcasted_iota(I32, shape, len(shape) - 2)


def brick_rows(index):
    return pl.ds(pl.multiple_of(index * SIDE, SIDE), SIDE)


def peers_of(subs):
    brick_at = lax.axis_index("brick")
    sub_at = lax.axis_index("sub")
    me = brick_at * subs + sub_at
    brick_step = jnp.where(brick_at % 2 == 0, subs, -subs)
    sub_step = jnp.where(sub_at % 2 == 0, 1, -1)
    return me, [me + brick_step, me - brick_step, me + sub_step, me - sub_step]


def route_kernel(subs, links_ref, table_ref, staged, sem):
    me, peers = peers_of(subs)
    links_row = links_ref[...]
    eye = (row_iota((BRK, BRK)) == lane_iota((BRK, BRK))).astype(F32)

    def turned(values):
        return lax.dot_general(
            eye, values.astype(F32), (((1,), (1,)), ((), ())), preferred_element_type=F32
        ).astype(I32)

    links_col = turned(links_row >> 8) * 256 + turned(links_row & 255)

    def keyed(links, own_face):
        key = jnp.full(links.shape, -1, I32)
        floor = jnp.full(links.shape, -1, I32)
        for number, peer in enumerate(peers):
            base = peer * FACES
            there = (links >= 0) & (links >= base) & (links < base + FACES)
            order = jnp.where(peer > me, own_face, links)
            key = jnp.where(there, order + number * 65536, key)
            floor = jnp.where(there, number * 65536, floor)
        return key, floor

    key_row, floor_row = keyed(links_row, lane_iota((6, BRK)) * 6 + row_iota((6, BRK)))
    key_col, floor_col = keyed(links_col, row_iota((BRK, 6)) * 6 + lane_iota((BRK, 6)))

    slot_lane = lane_iota((BRK, BRK))
    brick_sub = row_iota((BRK, BRK))
    listed = jnp.zeros((BRK, BRK), F32)
    odd = jnp.zeros((1, BRK), F32)
    for face in range(6):
        mine = key_col[:, face : face + 1]
        least = floor_col[:, face : face + 1]
        count = jnp.zeros((BRK, BRK), F32)
        for other in range(6):
            theirs = key_row[other : other + 1, :]
            count = count + ((theirs < mine) & (theirs >= least)).astype(F32)
        rank = jnp.sum(count, axis=1, keepdims=True).astype(I32)
        slot = jnp.where(mine >= 0, (least >> 16) * CAP + rank, -1)
        listed = listed + jnp.where(slot == slot_lane, (brick_sub + (face * BRK + 1)).astype(F32), 0.0)
        mine = key_row[face : face + 1, :]
        least = floor_row[face : face + 1, :]
        count = jnp.zeros((BRK, BRK), F32)
        for other in range(6):
            theirs = key_col[:, other : other + 1]
            count = count + ((theirs < mine) & (theirs >= least)).astype(F32)
        rank = jnp.sum(count, axis=0, keepdims=True).astype(I32)
        message = least >> 16
        place = native_place(face)
        if face // 2 == 0:
            plain = message < 2
        elif face // 2 == 2:
            plain = message >= 2
        else:
            plain = message < 0
        far = mine >= 0
        odd = odd + (far & jnp.logical_not(plain)).astype(F32)
        links = links_row[face : face + 1, :]
        local = links - me * FACES
        near = (links >= 0) & (local >= 0) & (local < FACES)
        near_brick = ((local - (face ^ 1)) * 10923) >> 16
        far_code = jnp.where(
            plain,
            (MESSAGE_BRICK + message) * SIDE + rank,
            (SLOT_BRICK + message * CAP + rank) * SIDE + place,
        )
        code = jnp.where(
            near, near_brick * SIDE + place, jnp.where(far, far_code, ZERO_BRICK * SIDE)
        )
        staged[face : face + 1, 0:BRK] = code
    staged[SEND_ROW : SEND_ROW + 1, 0:BRK] = jnp.sum(listed, axis=0, keepdims=True).astype(I32) - 1
    staged[ODD_ROW : ODD_ROW + 1, 0:BRK] = jnp.broadcast_to(
        jnp.sum(odd, axis=1, keepdims=True).astype(I32), (1, BRK)
    )
    copy = pltpu.make_async_copy(staged, table_ref, sem)
    copy.start()
    copy.wait()


def picker(shape, lane_axis, make):
    lane = lax.broadcasted_iota(I32, shape, lane_axis)
    inner = lax.broadcasted_iota(I32, shape, 1 - lane_axis)
    return make(lane, inner).astype(F32)


def exact_dot(left, right):
    return jnp.dot(left, right, precision=lax.Precision.HIGHEST, preferred_element_type=F32)


def column_rule(place):
    return lambda lane, inner: lane == inner * SIDE + place


def lanes_rule(place):
    return lambda lane, inner: lane == place * SIDE + inner


def fold_rule(lane, inner):
    return lane % SIDE == inner


def band_mask():
    return lane_iota((SIDE, PLANE)) // SIDE == row_iota((SIDE, PLANE))


def compacted(brick, rule):
    return exact_dot(brick, picker((PLANE, SIDE), 0, rule))


def spread(compact, rule):
    return exact_dot(compact, picker((SIDE, PLANE), 1, rule))


def compact_face(ref, brick, face):
    place = (face & 1) * (SIDE - 1)
    kind = face >> 1
    cells = ref[brick_rows(brick), :]
    row = ref[pl.ds(brick * SIDE + place, 1), :]
    from_x = compacted(cells, column_rule(place))
    from_y = compacted(cells, lanes_rule(place))
    from_z = compacted(jnp.where(band_mask(), row, 0.0), fold_rule)
    return jnp.where(kind == 0, from_x, jnp.where(kind == 1, from_y, from_z))


def fits(face, message):
    return face < 2 if message < 2 else face >= 4


def pack(ref, table, message, out_ref, base):
    if message < 2:
        column = lane_iota((SIDE, HALF)) % SIDE
        low = jnp.zeros((SIDE, HALF), F32)
        high = jnp.zeros((SIDE, HALF), F32)
        for slot in range(CAP):
            entry = jnp.maximum(table[SEND_ROW, message * CAP + slot], 0)
            rows = brick_rows(entry & (BRK - 1))
            turn = (slot - ((entry >> 6) & 1) * (SIDE - 1)) & (HALF - 1)
            here = column == slot
            low = jnp.where(here, pltpu.roll(ref[rows, 0:HALF], turn, 1), low)
            high = jnp.where(here, pltpu.roll(ref[rows, HALF:PLANE], turn, 1), high)
        out_ref[base : base + SIDE, 0:HALF] = low
        out_ref[base : base + SIDE, HALF:PLANE] = high
    else:
        for slot in range(CAP):
            entry = jnp.maximum(table[SEND_ROW, message * CAP + slot], 0)
            row = (entry & (BRK - 1)) * SIDE + ((entry >> 6) & 1) * (SIDE - 1)
            out_ref[base + slot : base + slot + 1, :] = ref[pl.ds(row, 1), :]

    @pl.when(table[ODD_ROW, 0] > 0)
    def _():
        def step(slot, carry):
            entry = table[SEND_ROW, message * CAP + slot]
            face = entry >> 6

            @pl.when((entry >= 0) & jnp.logical_not(fits(face, message)))
            def _():
                compact = compact_face(ref, entry & (BRK - 1), face)
                if message < 2:
                    cells = spread(compact, column_rule(slot))
                    here = lane_iota((SIDE, PLANE)) % SIDE == slot
                    out_ref[base : base + SIDE, :] = jnp.where(
                        here, cells, out_ref[base : base + SIDE, :]
                    )
                else:
                    cells = jnp.where(band_mask(), spread(compact, fold_rule), 0.0)
                    here = row_iota((SIDE, PLANE)) == slot
                    out_ref[base : base + SIDE, :] = jnp.where(
                        here, jnp.sum(cells, axis=0, keepdims=True), out_ref[base : base + SIDE, :]
                    )

            return carry

        lax.fori_loop(0, CAP, step, 0)


def fill_extended(ext, field_ref, messages, base, table):
    ext[0 : BRK * SIDE, :] = field_ref[...]
    ext[ZERO_BRICK * SIDE : (ZERO_BRICK + 1) * SIDE, :] = jnp.zeros((SIDE, PLANE), F32)
    for message in range(PEERS):
        at = (MESSAGE_BRICK + message) * SIDE
        ext[at : at + SIDE, :] = messages[message][base : base + SIDE, :]

    @pl.when(table[ODD_ROW, 0] > 0)
    def _():
        for message in range(PEERS):
            at = (MESSAGE_BRICK + message) * SIDE

            def step(slot, carry):
                entry = table[SEND_ROW, message * CAP + slot]
                face = entry >> 6

                @pl.when((entry >= 0) & jnp.logical_not(fits(face, message)))
                def _():
                    cells = ext[at : at + SIDE, :]
                    if message < 2:
                        compact = compacted(cells, column_rule(slot))
                    else:
                        row = jnp.sum(
                            jnp.where(row_iota((SIDE, PLANE)) == slot, cells, 0.0), axis=0, keepdims=True
                        )
                        compact = compacted(jnp.where(band_mask(), row, 0.0), fold_rule)
                    place = (1 - (face & 1)) * (SIDE - 1)
                    kind = face >> 1
                    from_x = spread(compact, column_rule(place))
                    from_y = spread(compact, lanes_rule(place))
                    row = jnp.where(band_mask(), spread(compact, fold_rule), 0.0)
                    from_z = jnp.broadcast_to(jnp.sum(row, axis=0, keepdims=True), (SIDE, PLANE))
                    ext[brick_rows(SLOT_BRICK + message * CAP + slot), :] = jnp.where(
                        kind == 0, from_x, jnp.where(kind == 1, from_y, from_z)
                    )

                return carry

            lax.fori_loop(0, CAP, step, 0)


def beside(ext, table, brick, low, high):
    lane = lane_iota((SIDE, HALF))
    column = lane % SIDE
    row = row_iota((SIDE, HALF))

    def entry(face):
        code = table[face, brick]
        return code >> 4, code & (SIDE - 1)

    source, place = entry(0)
    rows = brick_rows(source)
    turn = (HALF - place) & (HALF - 1)
    here = column == 0
    x_lower = (
        jnp.where(here, pltpu.roll(ext[rows, 0:HALF], turn, 1), pltpu.roll(low, 1, 1)),
        jnp.where(here, pltpu.roll(ext[rows, HALF:PLANE], turn, 1), pltpu.roll(high, 1, 1)),
    )
    source, place = entry(1)
    rows = brick_rows(source)
    turn = SIDE - 1 - place
    here = column == SIDE - 1
    x_upper = (
        jnp.where(here, pltpu.roll(ext[rows, 0:HALF], turn, 1), pltpu.roll(low, HALF - 1, 1)),
        jnp.where(here, pltpu.roll(ext[rows, HALF:PLANE], turn, 1), pltpu.roll(high, HALF - 1, 1)),
    )
    source, place = entry(2)
    part = pl.multiple_of((place >> 3) * HALF, HALF)
    turn = (HALF - (place & 7) * SIDE) & (HALF - 1)
    ghost = pltpu.roll(ext[brick_rows(source), pl.ds(part, HALF)], turn, 1)
    turned_low = pltpu.roll(low, SIDE, 1)
    turned_high = pltpu.roll(high, SIDE, 1)
    here = lane < SIDE
    y_lower = (jnp.where(here, ghost, turned_low), jnp.where(here, turned_low, turned_high))
    source, place = entry(3)
    part = pl.multiple_of((place >> 3) * HALF, HALF)
    turn = HALF - SIDE - (place & 7) * SIDE
    ghost = pltpu.roll(ext[brick_rows(source), pl.ds(part, HALF)], turn, 1)
    turned_low = pltpu.roll(low, HALF - SIDE, 1)
    turned_high = pltpu.roll(high, HALF - SIDE, 1)
    here = lane >= HALF - SIDE
    y_upper = (jnp.where(here, turned_high, turned_low), jnp.where(here, ghost, turned_high))
    source, place = entry(4)
    ghost = ext[pl.ds(source * SIDE + place, 1), :]
    here = row == 0
    z_lower = (
        jnp.where(here, ghost[:, 0:HALF], pltpu.roll(low, 1, 0)),
        jnp.where(here, ghost[:, HALF:PLANE], pltpu.roll(high, 1, 0)),
    )
    source, place = entry(5)
    ghost = ext[pl.ds(source * SIDE + place, 1), :]
    here = row == SIDE - 1
    z_upper = (
        jnp.where(here, ghost[:, 0:HALF], pltpu.roll(low, SIDE - 1, 0)),
        jnp.where(here, ghost[:, HALF:PLANE], pltpu.roll(high, SIDE - 1, 0)),
    )
    return [x_lower, x_upper, y_lower, y_upper, z_lower, z_upper]


LANES = (slice(0, HALF), slice(HALF, PLANE))
DIAGONAL = 6
SCALE = 7


def pack_kernel(table, field_ref, kappa_ref, *outs):
    for message in range(PEERS):
        pack(field_ref, table, message, outs[message], 0)
        pack(kappa_ref, table, message, outs[message], SIDE)


def first_kernel(table, field_ref, kappa_ref, source_ref, decay_ref, m0, m1, m2, m3, new_ref, coef_ref, o0, o1, o2, o3, ext, kappa_ext):
    messages = (m0, m1, m2, m3)
    fill_extended(ext, field_ref, messages, 0, table)
    fill_extended(kappa_ext, kappa_ref, messages, SIDE, table)

    def step(brick, carry):
        rows = brick_rows(brick)
        field = [ext[rows, lanes] for lanes in LANES]
        kappa = [kappa_ext[rows, lanes] for lanes in LANES]
        around = beside(ext, table, brick, *field)
        kappa_around = beside(kappa_ext, table, brick, *kappa)
        for half, lanes in enumerate(LANES):
            diagonal = decay_ref[rows, lanes]
            total = source_ref[rows, lanes]
            for face in range(6):
                link = 0.5 * (kappa[half] + kappa_around[face][half])
                coef_ref[face, rows, lanes] = link
                diagonal = diagonal + link
                total = total + link * around[face][half]
            scale = OMEGA / diagonal
            coef_ref[DIAGONAL, rows, lanes] = diagonal
            coef_ref[SCALE, rows, lanes] = scale
            new_ref[rows, lanes] = (1.0 - OMEGA) * field[half] + scale * total
        return carry

    lax.fori_loop(0, BRK, step, 0)
    for message, out in enumerate((o0, o1, o2, o3)):
        pack(new_ref, table, message, out, 0)


def sweep_kernel(table, field_ref, source_ref, coef_ref, m0, m1, m2, m3, new_ref, o0, o1, o2, o3, ext):
    fill_extended(ext, field_ref, (m0, m1, m2, m3), 0, table)

    def step(brick, carry):
        rows = brick_rows(brick)
        field = [ext[rows, lanes] for lanes in LANES]
        around = beside(ext, table, brick, *field)
        for half, lanes in enumerate(LANES):
            total = source_ref[rows, lanes]
            for face in range(6):
                total = total + coef_ref[face, rows, lanes] * around[face][half]
            new_ref[rows, lanes] = (1.0 - OMEGA) * field[half] + coef_ref[SCALE, rows, lanes] * total
        return carry

    lax.fori_loop(0, BRK, step, 0)
    for message, out in enumerate((o0, o1, o2, o3)):
        pack(new_ref, table, message, out, 0)


def restricted(*parts):
    rows = BRK * SIDE // 2
    paired = jnp.concatenate(
        [part[pl.ds(0, rows, stride=2), :] + part[pl.ds(1, rows, stride=2), :] for part in parts], axis=1
    )
    fine = lax.broadcasted_iota(I32, (PLANE, HALF), 0)
    target = lax.broadcasted_iota(I32, (PLANE, HALF), 1)
    same = (fine // (2 * SIDE) == target // SIDE) & ((fine % SIDE) // 2 == target % SIDE)
    table = jnp.where(same, 0.125, 0.0).astype(jnp.bfloat16)
    total = jnp.zeros((rows, HALF), F32)
    rest = paired
    for _ in range(3):
        part = rest.astype(jnp.bfloat16)
        total = total + jnp.dot(part, table, preferred_element_type=F32)
        rest = rest - part.astype(F32)
    return total


def coarse_tiles(values):
    depth = SIDE // 2
    for coarse in range(COARSE_DEV):
        cz, cy, cx = coarse // 4, coarse // 2 % 2, coarse % 2
        for pz in range(2):
            for py in range(2):
                fine = ((2 * cz + pz) * EDGE + 2 * cy + py) * EDGE + 2 * cx
                left = values[fine * depth : (fine + 1) * depth, :]
                right = values[(fine + 1) * depth : (fine + 2) * depth, :]
                yield coarse, pz, py, left + pltpu.roll(right, depth, 1)


def write_coarse(values, out_ref, base):
    for coarse, pz, py, tile in coarse_tiles(values):
        top = base + pz * (SIDE // 2)
        out_ref[coarse, top : top + SIDE // 2, py * HALF : (py + 1) * HALF] = tile


def coefficient_kernel(kappa_ref, decay_ref, out_ref, low, high):
    for ref, base in ((kappa_ref, 0), (decay_ref, SIDE)):
        low[...] = ref[:, 0:HALF]
        high[...] = ref[:, HALF:PLANE]
        write_coarse(restricted(low, high), out_ref, base)


def residual_kernel(table, wanted, field_ref, source_ref, coef_ref, coarse_ref, m0, m1, m2, m3, send_ref, ext, left_low, left_high, coarse_left):
    fill_extended(ext, field_ref, (m0, m1, m2, m3), 0, table)

    def step(brick, carry):
        rows = brick_rows(brick)
        field = [ext[rows, lanes] for lanes in LANES]
        around = beside(ext, table, brick, *field)
        for half, lanes in enumerate(LANES):
            total = source_ref[rows, lanes] - coef_ref[DIAGONAL, rows, lanes] * field[half]
            for face in range(6):
                total = total + coef_ref[face, rows, lanes] * around[face][half]
            (left_low, left_high)[half][rows, :] = total
        return carry

    lax.fori_loop(0, BRK, step, 0)
    write_coarse(restricted(left_low, left_high), coarse_left, 0)

    def hand_over(target, carry):
        chosen = jnp.maximum(wanted[target], 0)
        send_ref[target, 0:SIDE, :] = coarse_left[chosen]
        send_ref[target, SIDE : 3 * SIDE, :] = coarse_ref[chosen]
        return carry

    lax.fori_loop(0, send_ref.shape[0], hand_over, 0)


def place_kernel(per_row, coarse_source, arrived, out_ref, sem):
    copies = [
        pltpu.make_async_copy(arrived.at[coarse_source[slot] // per_row], out_ref.at[slot], sem.at[slot])
        for slot in range(COARSE_DEV)
    ]
    for copy in copies:
        copy.start()
    for copy in copies:
        copy.wait()


def paired(block, axis, offset):
    size = lax.axis_size(axis)
    route = []
    for first in range(offset, size + offset, 2):
        one, two = first % size, (first + 1) % size
        route += [(one, two), (two, one)]
    return lax.ppermute(block, axis, route)


def exchanged(outgoing):
    return [
        paired(outgoing[0], "brick", 0),
        paired(outgoing[1], "brick", 1),
        paired(outgoing[2], "sub", 0),
        paired(outgoing[3], "sub", 1),
    ]


VMEM_SPEC = pl.BlockSpec(memory_space=pltpu.VMEM)
SMEM_SPEC = pl.BlockSpec(memory_space=pltpu.SMEM)
ANY_SPEC = pl.BlockSpec(memory_space=pl.ANY)


def in_vmem(*shape):
    return pltpu.VMEM(shape, F32)


def kernel_call(kernel, name, ins, outs, out_specs=None, scratch=()):
    return pl.pallas_call(
        kernel,
        out_shape=outs,
        in_specs=ins,
        out_specs=out_specs if out_specs is not None else tuple(VMEM_SPEC for _ in outs),
        scratch_shapes=list(scratch),
        compiler_params=pltpu.CompilerParams(vmem_limit_bytes=VMEM_LIMIT),
        name=name,
    )


def body(field_start, source, diffusion, decay_rate, neighbour, coarse_source):
    subs = lax.axis_size("sub")
    rows = BRK * SIDE
    field_start, source, diffusion, decay_rate = (
        array.reshape(rows, PLANE) for array in (field_start, source, diffusion, decay_rate)
    )
    table = kernel_call(
        functools.partial(route_kernel, subs),
        "route",
        [VMEM_SPEC],
        jax.ShapeDtypeStruct((8, 128), I32),
        out_specs=SMEM_SPEC,
        scratch=[pltpu.VMEM((8, 128), I32), pltpu.SemaphoreType.DMA(())],
    )(neighbour.T)
    message = in_vmem(SIDE, PLANE)
    double = in_vmem(2 * SIDE, PLANE)
    extended = pltpu.VMEM((EXT_BRICKS * SIDE, PLANE), F32)

    outgoing = kernel_call(
        pack_kernel, "pack", [SMEM_SPEC] + [VMEM_SPEC] * 2, (double,) * PEERS
    )(table, field_start, diffusion)
    incoming = exchanged(outgoing)

    me = lax.axis_index("brick") * subs + lax.axis_index("sub")
    orders = lax.all_gather(coarse_source, "brick")
    mine = orders - me * COARSE_DEV
    mine = jnp.where((mine >= 0) & (mine < COARSE_DEV), mine, -1)
    wanted = jnp.max(mine, axis=1)
    coarse_coefs = kernel_call(
        coefficient_kernel, "coarse_coefficients", [VMEM_SPEC] * 2, (in_vmem(COARSE_DEV, 2 * SIDE, PLANE),),
        scratch=[pltpu.VMEM((rows, HALF), F32), pltpu.VMEM((rows, HALF), F32)],
    )(diffusion, decay_rate)[0]

    field, coefs, *outgoing = kernel_call(
        first_kernel,
        "first_sweep",
        [SMEM_SPEC] + [VMEM_SPEC] * 8,
        (in_vmem(rows, PLANE), in_vmem(8, rows, PLANE)) + (message,) * PEERS,
        scratch=[extended, extended],
    )(table, field_start, diffusion, source, decay_rate, *incoming)
    incoming = exchanged(outgoing)
    for _ in range(SWEEPS - 1):
        field, *outgoing = kernel_call(
            sweep_kernel,
            "next_sweep",
            [SMEM_SPEC] + [VMEM_SPEC] * 7,
            (in_vmem(rows, PLANE),) + (message,) * PEERS,
            scratch=[extended],
        )(table, field, source, coefs, *incoming)
        incoming = exchanged(outgoing)
    brick_count = lax.axis_size("brick")
    send = kernel_call(
        residual_kernel,
        "residual",
        [SMEM_SPEC] * 2 + [VMEM_SPEC] * 8,
        (in_vmem(brick_count, 3 * SIDE, PLANE),),
        scratch=[extended, pltpu.VMEM((rows, HALF), F32), pltpu.VMEM((rows, HALF), F32), pltpu.VMEM((COARSE_DEV, SIDE, PLANE), F32)],
    )(table, wanted, field, source, coefs, coarse_coefs, *incoming)[0]
    arrived = lax.all_to_all(send, "brick", split_axis=0, concat_axis=0, tiled=True)
    moved = kernel_call(
        functools.partial(place_kernel, subs * COARSE_DEV),
        "place",
        [SMEM_SPEC, ANY_SPEC],
        jax.ShapeDtypeStruct((COARSE_DEV, 3 * SIDE, PLANE), F32),
        out_specs=ANY_SPEC,
        scratch=[pltpu.SemaphoreType.DMA((COARSE_DEV,))],
    )(coarse_source, arrived)
    return field.reshape(BRK, SIDE, PLANE), moved.reshape(COARSE_DEV, 3, SIDE, PLANE)


def solution(mesh):
    placed = (
        P(("brick", "sub"), None, None),
        P(("brick", "sub"), None, None),
        P(("brick", "sub"), None, None),
        P(("brick", "sub"), None, None),
        P(("brick", "sub"), None),
        P(("brick", "sub")),
    )
    return jax.shard_map(
        body,
        mesh=mesh,
        in_specs=placed,
        out_specs=(P(("brick", "sub"), None, None), P(("brick", "sub"), None, None, None)),
        check_vma=False,
    )
```

```python
import functools

import jax
import jax.numpy as jnp
from jax import lax
from jax.experimental import pallas as pl
from jax.experimental.pallas import tpu as pltpu
from jax.sharding import PartitionSpec as P

EDGE = 4
LZ = 4
SWEEPS = 2
OMEGA = 0.8
UNROLL = 16

SIDE = 16
PLANE = SIDE * SIDE
HALF = PLANE // 2
BRK = EDGE * EDGE * LZ
FACES = 6 * BRK
COARSE_DEV = BRK // 8
CAP = 16
KNOWN_ROWS = 8
CHUNKS = 4
PEERS = 4
ZERO_BRICK = BRK
EXT_BRICKS = BRK + 1
SEND_ROW = 6
ODD_ROW = 7
F32 = jnp.float32
I32 = jnp.int32
VMEM_LIMIT = 16 * 1024 * 1024


def native_place(face):
    return SIDE - 1 if face % 2 == 0 else 0


def lane_iota(shape):
    return lax.broadcasted_iota(I32, shape, len(shape) - 1)


def row_iota(shape):
    return lax.broadcasted_iota(I32, shape, len(shape) - 2)


def brick_rows(index):
    return pl.ds(pl.multiple_of(index * SIDE, SIDE), SIDE)


def peers_of(subs):
    brick_at = lax.axis_index("brick")
    sub_at = lax.axis_index("sub")
    me = brick_at * subs + sub_at
    brick_step = jnp.where(brick_at % 2 == 0, subs, -subs)
    sub_step = jnp.where(sub_at % 2 == 0, 1, -1)
    return me, [me + brick_step, me - brick_step, me + sub_step, me - sub_step]


def route(subs, links_ref, table_ref, staged, sem):
    me, peers = peers_of(subs)
    links_row = links_ref[...]
    eye = (row_iota((BRK, BRK)) == lane_iota((BRK, BRK))).astype(F32)

    def turned(values):
        return lax.dot_general(
            eye, values.astype(F32), (((1,), (1,)), ((), ())), preferred_element_type=F32
        ).astype(I32)

    links_col = turned(links_row >> 8) * 256 + turned(links_row & 255)

    def keyed(links, own_face):
        key = jnp.full(links.shape, -1, I32)
        floor = jnp.full(links.shape, -1, I32)
        for number, peer in enumerate(peers):
            base = peer * FACES
            there = (links >= 0) & (links >= base) & (links < base + FACES)
            order = jnp.where(peer > me, own_face, links)
            key = jnp.where(there, order + number * 65536, key)
            floor = jnp.where(there, number * 65536, floor)
        return key, floor

    key_row, _ = keyed(links_row, lane_iota((6, BRK)) * 6 + row_iota((6, BRK)))
    key_col, floor_col = keyed(links_col, row_iota((BRK, 6)) * 6 + lane_iota((BRK, 6)))

    slot_lane = lane_iota((BRK, BRK))
    brick_sub = row_iota((BRK, BRK))
    listed = jnp.zeros((BRK, BRK), F32)
    odd = jnp.zeros((BRK, 1), F32)
    for face in range(6):
        mine = key_col[:, face : face + 1]
        least = floor_col[:, face : face + 1]
        count = jnp.zeros((BRK, BRK), F32)
        for other in range(6):
            theirs = key_row[other : other + 1, :]
            count = count + ((theirs < mine) & (theirs >= least)).astype(F32)
        rank = jnp.sum(count, axis=1, keepdims=True).astype(I32)
        slot = jnp.where(mine >= 0, (least >> 16) * CAP + rank, -1)
        listed = listed + jnp.where(slot == slot_lane, (brick_sub + (face * BRK + 1)).astype(F32), 0.0)
        message = least >> 16
        if face // 2 == 0:
            plain = message < 2
        elif face // 2 == 2:
            plain = message >= 2
        else:
            plain = message < 0
        odd = odd + ((mine >= 0) & jnp.logical_not(plain)).astype(F32)
        links = links_row[face : face + 1, :]
        local = links - me * FACES
        near = (links >= 0) & (local >= 0) & (local < FACES)
        near_brick = ((local - (face ^ 1)) * 10923) >> 16
        code = jnp.where(near, near_brick * SIDE + native_place(face), ZERO_BRICK * SIDE)
        staged[face : face + 1, 0:BRK] = code
    staged[SEND_ROW : SEND_ROW + 1, 0:BRK] = jnp.sum(listed, axis=0, keepdims=True).astype(I32) - 1
    staged[ODD_ROW : ODD_ROW + 1, 0:BRK] = jnp.broadcast_to(
        jnp.sum(odd, axis=0, keepdims=True).astype(I32), (1, BRK)
    )
    copy = pltpu.make_async_copy(staged, table_ref, sem)
    copy.start()
    copy.wait()


def picker(shape, lane_axis, make):
    lane = lax.broadcasted_iota(I32, shape, lane_axis)
    inner = lax.broadcasted_iota(I32, shape, 1 - lane_axis)
    return make(lane, inner).astype(F32)


def exact_dot(left, right):
    return jnp.dot(left, right, precision=lax.Precision.HIGHEST, preferred_element_type=F32)


def column_rule(place):
    return lambda lane, inner: lane == inner * SIDE + place


def lanes_rule(place):
    return lambda lane, inner: lane == place * SIDE + inner


def fold_rule(lane, inner):
    return lane % SIDE == inner


def band_mask():
    return lane_iota((SIDE, PLANE)) // SIDE == row_iota((SIDE, PLANE))


def compacted(brick, rule):
    return exact_dot(brick, picker((PLANE, SIDE), 0, rule))


def spread(compact, rule):
    return exact_dot(compact, picker((SIDE, PLANE), 1, rule))


def compact_face(ref, brick, face):
    place = (face & 1) * (SIDE - 1)
    kind = face >> 1
    cells = ref[brick_rows(brick), :]
    row = ref[pl.ds(brick * SIDE + place, 1), :]
    from_x = compacted(cells, column_rule(place))
    from_y = compacted(cells, lanes_rule(place))
    from_z = compacted(jnp.where(band_mask(), row, 0.0), fold_rule)
    return jnp.where(kind == 0, from_x, jnp.where(kind == 1, from_y, from_z))


def fits(face, message):
    return face < 2 if message < 2 else face >= 4


def pack(ref, table, message, out_ref, base):
    if message < 2:
        column = lane_iota((SIDE, HALF)) % SIDE
        low = jnp.zeros((SIDE, HALF), F32)
        high = jnp.zeros((SIDE, HALF), F32)
        for slot in range(CAP):
            entry = jnp.maximum(table[SEND_ROW, message * CAP + slot], 0)
            rows = brick_rows(entry & (BRK - 1))
            turn = (slot - ((entry >> 6) & 1) * (SIDE - 1)) & (HALF - 1)
            here = column == slot
            low = jnp.where(here, pltpu.roll(ref[rows, 0:HALF], turn, 1), low)
            high = jnp.where(here, pltpu.roll(ref[rows, HALF:PLANE], turn, 1), high)
        out_ref[base : base + SIDE, 0:HALF] = low
        out_ref[base : base + SIDE, HALF:PLANE] = high
    else:
        for slot in range(CAP):
            entry = jnp.maximum(table[SEND_ROW, message * CAP + slot], 0)
            row = (entry & (BRK - 1)) * SIDE + ((entry >> 6) & 1) * (SIDE - 1)
            out_ref[base + slot : base + slot + 1, :] = ref[pl.ds(row, 1), :]

    @pl.when(table[ODD_ROW, 0] > 0)
    def _():
        def step(slot, carry):
            entry = table[SEND_ROW, message * CAP + slot]
            face = entry >> 6

            @pl.when((entry >= 0) & jnp.logical_not(fits(face, message)))
            def _():
                compact = compact_face(ref, entry & (BRK - 1), face)
                if message < 2:
                    cells = spread(compact, column_rule(slot))
                    here = lane_iota((SIDE, PLANE)) % SIDE == slot
                    out_ref[base : base + SIDE, :] = jnp.where(
                        here, cells, out_ref[base : base + SIDE, :]
                    )
                else:
                    cells = jnp.where(band_mask(), spread(compact, fold_rule), 0.0)
                    here = row_iota((SIDE, PLANE)) == slot
                    out_ref[base : base + SIDE, :] = jnp.where(
                        here, jnp.sum(cells, axis=0, keepdims=True), out_ref[base : base + SIDE, :]
                    )

            return carry

        lax.fori_loop(0, CAP, step, 0)


def fill_extended(ext, field_ref):
    ext[0 : BRK * SIDE, :] = field_ref[...]
    ext[ZERO_BRICK * SIDE : (ZERO_BRICK + 1) * SIDE, :] = jnp.zeros((SIDE, PLANE), F32)


def from_peers(table, messages, bases, apply):
    column = lane_iota((SIDE, HALF)) % SIDE
    for message in range(2):
        cells = [[messages[message][base : base + SIDE, lanes] for lanes in LANES] for base in bases]
        for slot in range(CAP):
            entry = table[SEND_ROW, message * CAP + slot]
            valid = (entry >= 0) & fits(entry >> 6, message)
            entry = jnp.where(valid, entry, 0)
            face = entry >> 6
            place = face * (SIDE - 1)
            here = column == jnp.where(valid, place, -1)
            turn = (place - slot) & (HALF - 1)
            rows = brick_rows(entry & (BRK - 1))
            for half, lanes in enumerate(LANES):
                ghosts = [jnp.where(here, pltpu.roll(part[half], turn, 1), 0.0) for part in cells]
                apply(face, rows, lanes, ghosts)
    for message in range(2, PEERS):
        for slot in range(CAP):
            entry = table[SEND_ROW, message * CAP + slot]
            valid = (entry >= 0) & fits(entry >> 6, message)
            entry = jnp.where(valid, entry, 4 * BRK)
            face = entry >> 6
            rows = pl.ds((entry & (BRK - 1)) * SIDE + (face & 1) * (SIDE - 1), 1)
            ghosts = [
                jnp.where(valid, messages[message][base + slot : base + slot + 1, :], 0.0) for base in bases
            ]
            apply(face, rows, slice(0, PLANE), ghosts)

    @pl.when(table[ODD_ROW, 0] > 0)
    def _():
        for message in range(PEERS):

            def step(slot, carry):
                entry = table[SEND_ROW, message * CAP + slot]
                face = entry >> 6

                @pl.when((entry >= 0) & jnp.logical_not(fits(face, message)))
                def _():
                    ghosts = [
                        aligned(messages[message][base : base + SIDE, :], message, slot, face)
                        for base in bases
                    ]
                    apply(face, brick_rows(entry & (BRK - 1)), slice(0, PLANE), ghosts)

                return carry

            lax.fori_loop(0, CAP, step, 0)


def aligned(cells, message, slot, face):
    if message < 2:
        compact = compacted(cells, column_rule(slot))
    else:
        row = jnp.sum(jnp.where(row_iota((SIDE, PLANE)) == slot, cells, 0.0), axis=0, keepdims=True)
        compact = compacted(jnp.where(band_mask(), row, 0.0), fold_rule)
    place = (face & 1) * (SIDE - 1)
    kind = face >> 1
    from_x = spread(compact, column_rule(place))
    from_y = spread(compact, lanes_rule(place))
    row = jnp.where(band_mask(), spread(compact, fold_rule), 0.0)
    from_z = jnp.where(
        row_iota((SIDE, PLANE)) == place, jnp.sum(row, axis=0, keepdims=True), 0.0
    )
    return jnp.where(kind == 0, from_x, jnp.where(kind == 1, from_y, from_z))


def beside(ext, table, brick, low, high):
    lane = lane_iota((SIDE, HALF))
    column = lane % SIDE
    row = row_iota((SIDE, HALF))

    def entry(face):
        code = table[face, brick]
        return code >> 4, code & (SIDE - 1)

    source, place = entry(0)
    rows = brick_rows(source)
    turn = (HALF - place) & (HALF - 1)
    here = column == 0
    x_lower = (
        jnp.where(here, pltpu.roll(ext[rows, 0:HALF], turn, 1), pltpu.roll(low, 1, 1)),
        jnp.where(here, pltpu.roll(ext[rows, HALF:PLANE], turn, 1), pltpu.roll(high, 1, 1)),
    )
    source, place = entry(1)
    rows = brick_rows(source)
    turn = SIDE - 1 - place
    here = column == SIDE - 1
    x_upper = (
        jnp.where(here, pltpu.roll(ext[rows, 0:HALF], turn, 1), pltpu.roll(low, HALF - 1, 1)),
        jnp.where(here, pltpu.roll(ext[rows, HALF:PLANE], turn, 1), pltpu.roll(high, HALF - 1, 1)),
    )
    source, place = entry(2)
    part = pl.multiple_of((place >> 3) * HALF, HALF)
    turn = (HALF - (place & 7) * SIDE) & (HALF - 1)
    ghost = pltpu.roll(ext[brick_rows(source), pl.ds(part, HALF)], turn, 1)
    turned_low = pltpu.roll(low, SIDE, 1)
    turned_high = pltpu.roll(high, SIDE, 1)
    here = lane < SIDE
    y_lower = (jnp.where(here, ghost, turned_low), jnp.where(here, turned_low, turned_high))
    source, place = entry(3)
    part = pl.multiple_of((place >> 3) * HALF, HALF)
    turn = HALF - SIDE - (place & 7) * SIDE
    ghost = pltpu.roll(ext[brick_rows(source), pl.ds(part, HALF)], turn, 1)
    turned_low = pltpu.roll(low, HALF - SIDE, 1)
    turned_high = pltpu.roll(high, HALF - SIDE, 1)
    here = lane >= HALF - SIDE
    y_upper = (jnp.where(here, turned_high, turned_low), jnp.where(here, ghost, turned_high))
    source, place = entry(4)
    ghost = ext[pl.ds(source * SIDE + place, 1), :]
    here = row == 0
    z_lower = (
        jnp.where(here, ghost[:, 0:HALF], pltpu.roll(low, 1, 0)),
        jnp.where(here, ghost[:, HALF:PLANE], pltpu.roll(high, 1, 0)),
    )
    source, place = entry(5)
    ghost = ext[pl.ds(source * SIDE + place, 1), :]
    here = row == SIDE - 1
    z_upper = (
        jnp.where(here, ghost[:, 0:HALF], pltpu.roll(low, SIDE - 1, 0)),
        jnp.where(here, ghost[:, HALF:PLANE], pltpu.roll(high, SIDE - 1, 0)),
    )
    return [x_lower, x_upper, y_lower, y_upper, z_lower, z_upper]


LANES = (slice(0, HALF), slice(HALF, PLANE))


def write_known(known, outs, base):
    for out in outs[:2]:
        out[base : base + KNOWN_ROWS, 0:HALF] = known
        out[base : base + KNOWN_ROWS, HALF:PLANE] = jnp.zeros((KNOWN_ROWS, HALF), F32)


def learned(known, messages, base):
    for message in messages[:2]:
        known = jnp.maximum(known, message[base : base + KNOWN_ROWS, 0:HALF])
    return known
DIAGONAL = 6


def start_kernel(subs, wishes, links_ref, *refs):
    arrays, table, loaded, outs, known_ref = refs[:4], refs[4], refs[5:9], refs[9:13], refs[13]
    staged, table_sem, sems = refs[14:]
    part = BRK * SIDE // CHUNKS
    copies = []
    for number, (array, target) in enumerate(zip(arrays, loaded)):
        for chunk in range(CHUNKS):
            rows = pl.ds(chunk * part, part)
            copies.append(
                pltpu.make_async_copy(array.at[rows], target.at[rows], sems.at[number * CHUNKS + chunk])
            )
            copies[-1].start()
    lane = lane_iota((KNOWN_ROWS, HALF)) - lax.axis_index("brick") * COARSE_DEV
    known = jnp.full((KNOWN_ROWS, HALF), -1.0, F32)
    for slot in range(COARSE_DEV):
        known = jnp.where(lane == slot, wishes[slot].astype(F32), known)
    known_ref[...] = known
    write_known(known, outs, 2 * SIDE)
    route(subs, links_ref, table, staged, table_sem)
    for copy in copies[: 2 * CHUNKS]:
        copy.wait()
    for message in range(PEERS):
        pack(loaded[0], table, message, outs[message], 0)
        pack(loaded[1], table, message, outs[message], SIDE)
    for copy in copies[2 * CHUNKS :]:
        copy.wait()


def links_kernel(table, field_ref, kappa_ref, source_ref, decay_ref, coef_ref, total_ref, ext, kappa_ext):
    fill_extended(ext, field_ref)
    fill_extended(kappa_ext, kappa_ref)

    def step(brick, carry):
        rows = brick_rows(brick)
        field = [ext[rows, lanes] for lanes in LANES]
        kappa = [kappa_ext[rows, lanes] for lanes in LANES]
        around = beside(ext, table, brick, *field)
        kappa_around = beside(kappa_ext, table, brick, *kappa)
        for half, lanes in enumerate(LANES):
            diagonal = decay_ref[rows, lanes]
            total = source_ref[rows, lanes]
            for face in range(6):
                link = 0.5 * (kappa[half] + kappa_around[face][half])
                coef_ref[face, rows, lanes] = link
                diagonal = diagonal + link
                total = total + link * around[face][half]
            coef_ref[DIAGONAL, rows, lanes] = diagonal
            total_ref[rows, lanes] = total
        return carry

    lax.fori_loop(0, BRK, step, 0, unroll=UNROLL)


def first_kernel(table, coef_in, total_in, field_ref, known_ref, m0, m1, m2, m3, coef_ref, new_ref, scale_ref, now_known_ref, o0, o1, o2, o3):
    del coef_in, total_in
    messages = (m0, m1, m2, m3)
    known = learned(known_ref[...], messages, 2 * SIDE)
    now_known_ref[...] = known
    write_known(known, (o0, o1), SIDE)

    def apply(face, rows, lanes, ghosts):
        field, kappa = ghosts
        more = 0.5 * kappa
        link = coef_ref[face, rows, lanes] + more
        coef_ref[face, rows, lanes] = link
        coef_ref[DIAGONAL, rows, lanes] += more
        new_ref[rows, lanes] += link * field

    from_peers(table, messages, (0, SIDE), apply)

    def step(brick, carry):
        rows = brick_rows(brick)
        scale = OMEGA / coef_ref[DIAGONAL, rows, :]
        scale_ref[rows, :] = scale
        new_ref[rows, :] = (1.0 - OMEGA) * field_ref[rows, :] + scale * new_ref[rows, :]
        return carry

    lax.fori_loop(0, BRK, step, 0, unroll=UNROLL)
    for message, out in enumerate((o0, o1, o2, o3)):
        pack(new_ref, table, message, out, 0)


def sweep_kernel(table, field_ref, source_ref, coef_ref, scale_ref, new_ref, ext):
    fill_extended(ext, field_ref)

    def step(brick, carry):
        rows = brick_rows(brick)
        field = [ext[rows, lanes] for lanes in LANES]
        around = beside(ext, table, brick, *field)
        for half, lanes in enumerate(LANES):
            total = source_ref[rows, lanes]
            for face in range(6):
                total = total + coef_ref[face, rows, lanes] * around[face][half]
            new_ref[rows, lanes] = (1.0 - OMEGA) * field[half] + scale_ref[rows, lanes] * total
        return carry

    lax.fori_loop(0, BRK, step, 0, unroll=UNROLL)


def sweep_rest_kernel(table, new_in, coef_ref, scale_ref, known_ref, m0, m1, m2, m3, new_ref, now_known_ref, o0, o1, o2, o3):
    del new_in
    messages = (m0, m1, m2, m3)
    known = learned(known_ref[...], messages, SIDE)
    now_known_ref[...] = known
    write_known(known, (o0, o1), SIDE)

    def apply(face, rows, lanes, ghosts):
        new_ref[rows, lanes] += scale_ref[rows, lanes] * (coef_ref[face, rows, lanes] * ghosts[0])

    from_peers(table, messages, (0,), apply)
    for message, out in enumerate((o0, o1, o2, o3)):
        pack(new_ref, table, message, out, 0)


def residual_kernel(table, field_ref, source_ref, coef_ref, left_low, left_high, field_out, ext, sem):
    copy = pltpu.make_async_copy(field_ref, field_out, sem)
    copy.start()
    fill_extended(ext, field_ref)

    def step(brick, carry):
        rows = brick_rows(brick)
        field = [ext[rows, lanes] for lanes in LANES]
        around = beside(ext, table, brick, *field)
        for half, lanes in enumerate(LANES):
            total = source_ref[rows, lanes] - coef_ref[DIAGONAL, rows, lanes] * field[half]
            for face in range(6):
                total = total + coef_ref[face, rows, lanes] * around[face][half]
            (left_low, left_high)[half][rows, :] = total
        return carry

    lax.fori_loop(0, BRK, step, 0, unroll=UNROLL)
    copy.wait()


def residual_rest_kernel(table, low_in, high_in, coef_ref, m0, m1, m2, m3, left_low, left_high, coarse_left):
    del low_in, high_in

    def apply(face, rows, lanes, ghosts):
        more = coef_ref[face, rows, lanes] * ghosts[0]
        if lanes != LANES[1]:
            left_low[rows, :] += more[:, 0:HALF]
        if lanes != LANES[0]:
            left_high[rows, :] += more[:, more.shape[1] - HALF :]

    from_peers(table, (m0, m1, m2, m3), (0,), apply)
    write_coarse(restricted(left_low, left_high), coarse_left, 0)


def restricted(*parts):
    rows = BRK * SIDE // 2
    paired = jnp.concatenate(
        [part[pl.ds(0, rows, stride=2), :] + part[pl.ds(1, rows, stride=2), :] for part in parts], axis=1
    )
    fine = lax.broadcasted_iota(I32, (PLANE, HALF), 0)
    target = lax.broadcasted_iota(I32, (PLANE, HALF), 1)
    same = (fine // (2 * SIDE) == target // SIDE) & ((fine % SIDE) // 2 == target % SIDE)
    table = jnp.where(same, 0.125, 0.0).astype(jnp.bfloat16)
    total = jnp.zeros((rows, HALF), F32)
    rest = paired
    for _ in range(3):
        part = rest.astype(jnp.bfloat16)
        total = total + jnp.dot(part, table, preferred_element_type=F32)
        rest = rest - part.astype(F32)
    return total


def coarse_tiles(values):
    depth = SIDE // 2
    for coarse in range(COARSE_DEV):
        cz, cy, cx = coarse // 4, coarse // 2 % 2, coarse % 2
        for pz in range(2):
            for py in range(2):
                fine = ((2 * cz + pz) * EDGE + 2 * cy + py) * EDGE + 2 * cx
                left = values[fine * depth : (fine + 1) * depth, :]
                right = values[(fine + 1) * depth : (fine + 2) * depth, :]
                yield coarse, pz, py, left + pltpu.roll(right, depth, 1)


def write_coarse(values, out_ref, base):
    for coarse, pz, py, tile in coarse_tiles(values):
        top = base + pz * (SIDE // 2)
        out_ref[coarse, top : top + SIDE // 2, py * HALF : (py + 1) * HALF] = tile


def coefficient_kernel(kappa_ref, decay_ref, out_ref, low, high):
    for ref, base in ((kappa_ref, 0), (decay_ref, SIDE)):
        low[...] = ref[:, 0:HALF]
        high[...] = ref[:, HALF:PLANE]
        write_coarse(restricted(low, high), out_ref, base)


def hand_over_kernel(subs, known_ref, e0, e1, m0, m1, coarse_left, coarse_coefs, send_ref, held, wanted, sem):
    known = learned(jnp.maximum(known_ref[...], jnp.maximum(e0[...], e1[...])), (m0, m1), SIDE)
    mine = known.astype(I32) - (lax.axis_index("brick") * subs + lax.axis_index("sub")) * COARSE_DEV
    mine = jnp.where((mine >= 0) & (mine < COARSE_DEV), mine + 1, 0)
    for reach in (1, 2, 4):
        mine = mine + pltpu.roll(mine, HALF - reach, 1)
    held[...] = mine
    copy = pltpu.make_async_copy(held, wanted, sem)
    copy.start()
    copy.wait()
    for target in range(send_ref.shape[0]):
        chosen = jnp.maximum(wanted[0, target * COARSE_DEV] - 1, 0)
        send_ref[target, 0:SIDE, :] = coarse_left[chosen]
        send_ref[target, SIDE : 3 * SIDE, :] = coarse_coefs[chosen]


def place_kernel(per_row, coarse_source, arrived, out_ref, sem):
    copies = [
        pltpu.make_async_copy(arrived.at[coarse_source[slot] // per_row], out_ref.at[slot], sem.at[slot])
        for slot in range(COARSE_DEV)
    ]
    for copy in copies:
        copy.start()
    for copy in copies:
        copy.wait()


def paired(block, axis, offset):
    size = lax.axis_size(axis)
    route = []
    for first in range(offset, size + offset, 2):
        one, two = first % size, (first + 1) % size
        route += [(one, two), (two, one)]
    return lax.ppermute(block, axis, route)


def shifted(block, axis, distance):
    size = lax.axis_size(axis)
    return lax.ppermute(block, axis, [(place, (place + distance) % size) for place in range(size)])


def exchanged(outgoing):
    return [
        paired(outgoing[0], "brick", 0),
        paired(outgoing[1], "brick", 1),
        paired(outgoing[2], "sub", 0),
        paired(outgoing[3], "sub", 1),
    ]


VMEM_SPEC = pl.BlockSpec(memory_space=pltpu.VMEM)
SMEM_SPEC = pl.BlockSpec(memory_space=pltpu.SMEM)
HBM_SPEC = pl.BlockSpec(memory_space=pltpu.HBM)


def in_vmem(*shape):
    return pltpu.VMEM(shape, F32)


def kernel_call(kernel, name, ins, outs, out_specs=None, scratch=(), aliases=None):
    return pl.pallas_call(
        kernel,
        out_shape=outs,
        in_specs=ins,
        out_specs=out_specs if out_specs is not None else tuple(VMEM_SPEC for _ in outs),
        scratch_shapes=list(scratch),
        input_output_aliases=aliases or {},
        compiler_params=pltpu.CompilerParams(vmem_limit_bytes=VMEM_LIMIT),
        name=name,
    )


def body(field_start, source, diffusion, decay_rate, neighbour, coarse_source):
    subs = lax.axis_size("sub")
    rows = BRK * SIDE
    field_start, source, diffusion, decay_rate = (
        array.reshape(rows, PLANE) for array in (field_start, source, diffusion, decay_rate)
    )
    known_shape = in_vmem(KNOWN_ROWS, HALF)
    whole = in_vmem(rows, PLANE)
    message = (in_vmem(SIDE + KNOWN_ROWS, PLANE),) * 2 + (in_vmem(SIDE, PLANE),) * 2
    double = (in_vmem(2 * SIDE + KNOWN_ROWS, PLANE),) * 2 + (in_vmem(2 * SIDE, PLANE),) * 2
    extended = pltpu.VMEM((EXT_BRICKS * SIDE, PLANE), F32)

    table, field_start, diffusion, source, decay_rate, *outgoing, known = kernel_call(
        functools.partial(start_kernel, subs),
        "route_and_pack",
        [SMEM_SPEC, VMEM_SPEC] + [HBM_SPEC] * 4,
        (jax.ShapeDtypeStruct((8, 128), I32),) + (in_vmem(rows, PLANE),) * 4 + double + (known_shape,),
        out_specs=(SMEM_SPEC,) + (VMEM_SPEC,) * 9,
        scratch=[
            pltpu.VMEM((8, 128), I32),
            pltpu.SemaphoreType.DMA(()),
            pltpu.SemaphoreType.DMA((4 * CHUNKS,)),
        ],
    )(coarse_source, neighbour.T, *(pltpu.with_memory_space_constraint(a, pltpu.HBM) for a in (field_start, diffusion, source, decay_rate)))
    incoming = exchanged(outgoing)

    coarse_coefs = kernel_call(
        coefficient_kernel, "coarse_coefficients", [VMEM_SPEC] * 2, (in_vmem(COARSE_DEV, 2 * SIDE, PLANE),),
        scratch=[pltpu.VMEM((rows, HALF), F32), pltpu.VMEM((rows, HALF), F32)],
    )(diffusion, decay_rate)[0]

    coefs, total = kernel_call(
        links_kernel,
        "links",
        [SMEM_SPEC] + [VMEM_SPEC] * 4,
        (in_vmem(7, rows, PLANE), whole),
        scratch=[extended, extended],
    )(table, field_start, diffusion, source, decay_rate)
    coefs, field, scale, known, *outgoing = kernel_call(
        first_kernel,
        "first_sweep",
        [SMEM_SPEC] + [VMEM_SPEC] * 8,
        (in_vmem(7, rows, PLANE), whole, whole, known_shape) + message,
        aliases={1: 0, 2: 1},
    )(table, coefs, total, field_start, known, *incoming)
    incoming = exchanged(outgoing)
    for _ in range(SWEEPS - 1):
        field = kernel_call(
            sweep_kernel,
            "next_sweep",
            [SMEM_SPEC] + [VMEM_SPEC] * 4,
            (whole,),
            scratch=[extended],
        )(table, field, source, coefs, scale)[0]
        field, known, *outgoing = kernel_call(
            sweep_rest_kernel,
            "next_sweep_rest",
            [SMEM_SPEC] + [VMEM_SPEC] * 8,
            (whole, known_shape) + message,
            aliases={1: 0},
        )(table, field, coefs, scale, known, *incoming)
        incoming = exchanged(outgoing)
    others = [shifted(known, "brick", 6), shifted(known, "brick", -5)]
    left = in_vmem(rows, HALF)
    left_low, left_high, field = kernel_call(
        residual_kernel,
        "residual",
        [SMEM_SPEC] + [VMEM_SPEC] * 3,
        (left, left, jax.ShapeDtypeStruct((rows, PLANE), F32)),
        out_specs=(VMEM_SPEC, VMEM_SPEC, HBM_SPEC),
        scratch=[extended, pltpu.SemaphoreType.DMA(())],
    )(table, field, source, coefs)
    _, _, coarse_left = kernel_call(
        residual_rest_kernel,
        "residual_rest",
        [SMEM_SPEC] + [VMEM_SPEC] * 7,
        (left, left, in_vmem(COARSE_DEV, SIDE, PLANE)),
        aliases={1: 0, 2: 1},
    )(table, left_low, left_high, coefs, *incoming)
    send = kernel_call(
        functools.partial(hand_over_kernel, subs),
        "hand_over",
        [VMEM_SPEC] * 7,
        (in_vmem(lax.axis_size("brick"), 3 * SIDE, PLANE),),
        scratch=[
            pltpu.VMEM((KNOWN_ROWS, HALF), I32),
            pltpu.SMEM((KNOWN_ROWS, HALF), I32),
            pltpu.SemaphoreType.DMA(()),
        ],
    )(known, *others, *incoming[:2], coarse_left, coarse_coefs)[0]
    arrived = lax.all_to_all(send, "brick", split_axis=0, concat_axis=0, tiled=True)
    moved = kernel_call(
        functools.partial(place_kernel, subs * COARSE_DEV),
        "place",
        [SMEM_SPEC, HBM_SPEC],
        jax.ShapeDtypeStruct((COARSE_DEV, 3 * SIDE, PLANE), F32),
        out_specs=HBM_SPEC,
        scratch=[pltpu.SemaphoreType.DMA((COARSE_DEV,))],
    )(coarse_source, arrived)
    return field.reshape(BRK, SIDE, PLANE), moved.reshape(COARSE_DEV, 3, SIDE, PLANE)


def solution(mesh):
    placed = (
        P(("brick", "sub"), None, None),
        P(("brick", "sub"), None, None),
        P(("brick", "sub"), None, None),
        P(("brick", "sub"), None, None),
        P(("brick", "sub"), None),
        P(("brick", "sub")),
    )
    return jax.shard_map(
        body,
        mesh=mesh,
        in_specs=placed,
        out_specs=(P(("brick", "sub"), None, None), P(("brick", "sub"), None, None, None)),
        check_vma=False,
    )
```

```python
import functools

import jax
import jax.numpy as jnp
from jax import lax
from jax.experimental import pallas as pl
from jax.experimental.pallas import tpu as pltpu
from jax.sharding import PartitionSpec as P

EDGE = 4
LZ = 4
SWEEPS = 2
OMEGA = 0.8
UNROLL = 16

SIDE = 16
PLANE = SIDE * SIDE
HALF = PLANE // 2
DEEP = SIDE // 2
BRK = EDGE * EDGE * LZ
FACES = 6 * BRK
COARSE_DEV = BRK // 8
CAP = 16
KNOWN_ROWS = 8
CHUNKS = 4
PEERS = 4
ZERO_BRICK = BRK
EXT_BRICKS = BRK + 1
LANES = (slice(0, HALF), slice(HALF, PLANE))
SEND_ROW = 6
ODD_ROW = 7
F32 = jnp.float32
I32 = jnp.int32
VMEM_LIMIT = 16 * 1024 * 1024


def lane_iota(shape):
    return lax.broadcasted_iota(I32, shape, len(shape) - 1)


def row_iota(shape):
    return lax.broadcasted_iota(I32, shape, len(shape) - 2)


def brick_rows(index):
    return pl.ds(pl.multiple_of(index * SIDE, SIDE), SIDE)


def peers_of(subs):
    brick_at = lax.axis_index("brick")
    sub_at = lax.axis_index("sub")
    me = brick_at * subs + sub_at
    brick_step = jnp.where(brick_at % 2 == 0, subs, -subs)
    sub_step = jnp.where(sub_at % 2 == 0, 1, -1)
    return me, [me + brick_step, me - brick_step, me + sub_step, me - sub_step]


def route(subs, links_ref, table_ref, staged, sem):
    me, peers = peers_of(subs)
    links_row = links_ref[...]
    eye = (row_iota((BRK, BRK)) == lane_iota((BRK, BRK))).astype(F32)

    def turned(values):
        return lax.dot_general(
            eye, values.astype(F32), (((1,), (1,)), ((), ())), preferred_element_type=F32
        ).astype(I32)

    links_col = turned(links_row >> 8) * 256 + turned(links_row & 255)

    def keyed(links, own_face):
        key = jnp.full(links.shape, -1, I32)
        floor = jnp.full(links.shape, -1, I32)
        for number, peer in enumerate(peers):
            base = peer * FACES
            there = (links >= 0) & (links >= base) & (links < base + FACES)
            order = jnp.where(peer > me, own_face, links)
            key = jnp.where(there, order + number * 65536, key)
            floor = jnp.where(there, number * 65536, floor)
        return key, floor

    key_row, _ = keyed(links_row, lane_iota((6, BRK)) * 6 + row_iota((6, BRK)))
    key_col, floor_col = keyed(links_col, row_iota((BRK, 6)) * 6 + lane_iota((BRK, 6)))

    slot_lane = lane_iota((BRK, BRK))
    brick_sub = row_iota((BRK, BRK))
    listed = jnp.zeros((BRK, BRK), F32)
    odd = jnp.zeros((BRK, 1), F32)
    for face in range(6):
        mine = key_col[:, face : face + 1]
        least = floor_col[:, face : face + 1]
        count = jnp.zeros((BRK, BRK), F32)
        for other in range(6):
            theirs = key_row[other : other + 1, :]
            count = count + ((theirs < mine) & (theirs >= least)).astype(F32)
        rank = jnp.sum(count, axis=1, keepdims=True).astype(I32)
        slot = jnp.where(mine >= 0, (least >> 16) * CAP + rank, -1)
        listed = listed + jnp.where(slot == slot_lane, (brick_sub + (face * BRK + 1)).astype(F32), 0.0)
        message = least >> 16
        if face // 2 == 0:
            plain = message < 2
        elif face // 2 == 2:
            plain = message >= 2
        else:
            plain = message < 0
        odd = odd + ((mine >= 0) & jnp.logical_not(plain)).astype(F32)
        links = links_row[face : face + 1, :]
        local = links - me * FACES
        near = (links >= 0) & (local >= 0) & (local < FACES)
        near_brick = ((local - (face ^ 1)) * 10923) >> 16
        code = jnp.where(near, near_brick, ZERO_BRICK)
        staged[face : face + 1, 0:BRK] = code
    staged[SEND_ROW : SEND_ROW + 1, 0:BRK] = jnp.sum(listed, axis=0, keepdims=True).astype(I32) - 1
    staged[ODD_ROW : ODD_ROW + 1, 0:BRK] = jnp.broadcast_to(
        jnp.sum(odd, axis=0, keepdims=True).astype(I32), (1, BRK)
    )
    copy = pltpu.make_async_copy(staged, table_ref, sem)
    copy.start()
    return copy


def picker(shape, lane_axis, make):
    lane = lax.broadcasted_iota(I32, shape, lane_axis)
    inner = lax.broadcasted_iota(I32, shape, 1 - lane_axis)
    return make(lane, inner).astype(F32)


def exact_dot(left, right):
    return jnp.dot(left, right, precision=lax.Precision.HIGHEST, preferred_element_type=F32)


def column_rule(place):
    return lambda lane, inner: lane == inner * SIDE + place


def lanes_rule(place):
    return lambda lane, inner: lane == place * SIDE + inner


def fold_rule(lane, inner):
    return lane % SIDE == inner


def band_mask():
    return lane_iota((SIDE, PLANE)) // SIDE == row_iota((SIDE, PLANE))


def compacted(brick, rule):
    return exact_dot(brick, picker((PLANE, SIDE), 0, rule))


def spread(compact, rule):
    return exact_dot(compact, picker((SIDE, PLANE), 1, rule))


def compact_face(ref, brick, face):
    place = (face & 1) * (SIDE - 1)
    kind = face >> 1
    cells = ref[brick_rows(brick), :]
    row = ref[pl.ds(brick * SIDE + place, 1), :]
    from_x = compacted(cells, column_rule(place))
    from_y = compacted(cells, lanes_rule(place))
    from_z = compacted(jnp.where(band_mask(), row, 0.0), fold_rule)
    return jnp.where(kind == 0, from_x, jnp.where(kind == 1, from_y, from_z))


def fits(face, message):
    return face < 2 if message < 2 else face >= 4


def pack(fields, table, message, out_ref):
    entries = [jnp.maximum(table[SEND_ROW, message * CAP + slot], 0) for slot in range(CAP)]
    if message < 2:
        column = lane_iota((SIDE, HALF)) % SIDE
        parts = [[jnp.zeros((SIDE, HALF), F32)] * 2 for _ in fields]
        for slot, entry in enumerate(entries):
            rows = brick_rows(entry & (BRK - 1))
            turn = (slot - ((entry >> 6) & 1) * (SIDE - 1)) & (HALF - 1)
            here = column == slot
            for ref, halves in zip(fields, parts):
                for half, lanes in enumerate(LANES):
                    halves[half] = jnp.where(here, pltpu.roll(ref[rows, lanes], turn, 1), halves[half])
        for number, halves in enumerate(parts):
            for half, lanes in enumerate(LANES):
                out_ref[number * SIDE : (number + 1) * SIDE, lanes] = halves[half]
    else:
        found = []
        for ref in fields:
            for entry in entries:
                row = (entry & (BRK - 1)) * SIDE + ((entry >> 6) & 1) * (SIDE - 1)
                found.append(ref[pl.ds(row, 1), :])
        for number, row in enumerate(found):
            out_ref[number : number + 1, :] = row

    for number, ref in enumerate(fields):
        pack_odd(ref, table, message, out_ref, number * SIDE)


def pack_odd(ref, table, message, out_ref, base):
    @pl.when(table[ODD_ROW, 0] > 0)
    def _():
        def step(slot, carry):
            entry = table[SEND_ROW, message * CAP + slot]
            face = entry >> 6

            @pl.when((entry >= 0) & jnp.logical_not(fits(face, message)))
            def _():
                compact = compact_face(ref, entry & (BRK - 1), face)
                if message < 2:
                    cells = spread(compact, column_rule(slot))
                    here = lane_iota((SIDE, PLANE)) % SIDE == slot
                    out_ref[base : base + SIDE, :] = jnp.where(
                        here, cells, out_ref[base : base + SIDE, :]
                    )
                else:
                    cells = jnp.where(band_mask(), spread(compact, fold_rule), 0.0)
                    here = row_iota((SIDE, PLANE)) == slot
                    out_ref[base : base + SIDE, :] = jnp.where(
                        here, jnp.sum(cells, axis=0, keepdims=True), out_ref[base : base + SIDE, :]
                    )

            return carry

        lax.fori_loop(0, CAP, step, 0)


def fill_extended(ext, field_ref):
    ext[0 : BRK * SIDE, :] = field_ref[...]
    ext[ZERO_BRICK * SIDE : (ZERO_BRICK + 1) * SIDE, :] = jnp.zeros((SIDE, PLANE), F32)


def from_peers(table, given, apply):
    column = lane_iota((SIDE, HALF)) % SIDE
    for message in range(2):
        cells = [[array[:, lanes] for lanes in LANES] for array in given[message]]
        for slot in range(CAP):
            entry = table[SEND_ROW, message * CAP + slot]
            valid = (entry >= 0) & fits(entry >> 6, message)
            entry = jnp.where(valid, entry, 0)
            place = (entry >> 6) * (SIDE - 1)
            here = column == jnp.where(valid, place, -1)
            turn = (place - slot) & (HALF - 1)
            rows = brick_rows(entry & (BRK - 1))
            for half, lanes in enumerate(LANES):
                values = [jnp.where(here, pltpu.roll(part[half], turn, 1), 0.0) for part in cells]
                apply(rows, lanes, values)
    for message in range(2, PEERS):
        for slot in range(CAP):
            entry = table[SEND_ROW, message * CAP + slot]
            valid = (entry >= 0) & fits(entry >> 6, message)
            entry = jnp.where(valid, entry, 0)
            rows = pl.ds((entry & (BRK - 1)) * SIDE + ((entry >> 6) & 1) * (SIDE - 1), 1)
            values = [jnp.where(valid, array[slot : slot + 1, :], 0.0) for array in given[message]]
            apply(rows, slice(0, PLANE), values)

    @pl.when(table[ODD_ROW, 0] > 0)
    def _():
        for message in range(PEERS):

            def step(slot, carry):
                entry = table[SEND_ROW, message * CAP + slot]
                face = entry >> 6

                @pl.when((entry >= 0) & jnp.logical_not(fits(face, message)))
                def _():
                    values = [aligned(array, message, slot, face) for array in given[message]]
                    apply(brick_rows(entry & (BRK - 1)), slice(0, PLANE), values)

                return carry

            lax.fori_loop(0, CAP, step, 0)


def aligned(cells, message, slot, face):
    if message < 2:
        compact = compacted(cells, column_rule(slot))
    else:
        row = jnp.sum(jnp.where(row_iota((SIDE, PLANE)) == slot, cells, 0.0), axis=0, keepdims=True)
        compact = compacted(jnp.where(band_mask(), row, 0.0), fold_rule)
    place = (face & 1) * (SIDE - 1)
    kind = face >> 1
    from_x = spread(compact, column_rule(place))
    from_y = spread(compact, lanes_rule(place))
    row = jnp.where(band_mask(), spread(compact, fold_rule), 0.0)
    from_z = jnp.where(
        row_iota((SIDE, PLANE)) == place, jnp.sum(row, axis=0, keepdims=True), 0.0
    )
    return jnp.where(kind == 0, from_x, jnp.where(kind == 1, from_y, from_z))


def beside(ext, table, brick, low, high):
    lane = lane_iota((SIDE, HALF))
    column = lane % SIDE
    row = row_iota((DEEP, HALF))

    def across(face):
        rows = brick_rows(table[face, brick])
        return ext[rows, 0:HALF], ext[rows, HALF:PLANE]

    def taken(cells, lanes):
        return jnp.take_along_axis(cells, lanes, axis=1)

    here = column == SIDE - 1
    lanes = jnp.where(column == 0, lane + (SIDE - 1), lane - 1)
    x_lower = [taken(jnp.where(here, far, own), lanes) for far, own in zip(across(0), (low, high))]
    here = column == 0
    lanes = jnp.where(column == SIDE - 1, lane - (SIDE - 1), lane + 1)
    x_upper = [taken(jnp.where(here, far, own), lanes) for far, own in zip(across(1), (low, high))]
    here = lane >= HALF - SIDE
    y_lower = [
        pltpu.roll(jnp.where(here, far, own), SIDE, 1)
        for far, own in ((across(2)[1], low), (low, high))
    ]
    here = lane < SIDE
    y_upper = [
        pltpu.roll(jnp.where(here, far, own), HALF - SIDE, 1)
        for far, own in ((high, low), (across(3)[0], high))
    ]
    below = pl.ds(pl.multiple_of(table[4, brick] * SIDE + DEEP, DEEP), DEEP)
    above = pl.ds(pl.multiple_of(table[5, brick] * SIDE, DEEP), DEEP)
    last = row == DEEP - 1
    first = row == 0
    z_lower, z_upper = [], []
    for own, lanes in zip((low, high), LANES):
        top, bottom = own[0:DEEP], own[DEEP:SIDE]
        z_lower.append(pltpu.roll(jnp.concatenate([top, jnp.where(last, ext[below, lanes], bottom)], axis=0), 1, 0))
        z_upper.append(
            pltpu.roll(jnp.concatenate([jnp.where(first, ext[above, lanes], top), bottom], axis=0), SIDE - 1, 0)
        )
    return [x_lower, x_upper, y_lower, y_upper, z_lower, z_upper]


def write_known(known, outs, base):
    for out in outs[:2]:
        out[base : base + KNOWN_ROWS, 0:HALF] = known
        out[base : base + KNOWN_ROWS, HALF:PLANE] = jnp.zeros((KNOWN_ROWS, HALF), F32)


def learned(known, messages, base, others=()):
    for other in others:
        known = jnp.maximum(known, other[...])
    for message in messages[:2]:
        known = jnp.maximum(known, message[base : base + KNOWN_ROWS, 0:HALF])
    return known


def chunked_copies(pairs, sems):
    part = BRK * SIDE // CHUNKS
    copies = []
    for chunk in range(CHUNKS):
        rows = pl.ds(chunk * part, part)
        for array, target in pairs:
            copies.append(pltpu.make_async_copy(array.at[rows], target.at[rows], sems.at[len(copies)]))
    return copies


def start_kernel(subs, wishes_hbm, links_hbm, field_hbm, kappa_hbm, table, field, kappa, o0, o1, o2, o3, known_ref, staged, wishes, links, wish_sem, link_sem, table_sem, sems):
    outs = (o0, o1, o2, o3)
    link_copy = pltpu.make_async_copy(links_hbm, links, link_sem)
    link_copy.start()
    wish_copy = pltpu.make_async_copy(wishes_hbm, wishes, wish_sem)
    wish_copy.start()
    copies = chunked_copies(((field_hbm, field), (kappa_hbm, kappa)), sems)
    for copy in copies:
        copy.start()
    link_copy.wait()
    table_copy = route(subs, links, table, staged, table_sem)
    wish_copy.wait()
    lane = lane_iota((KNOWN_ROWS, HALF)) - lax.axis_index("brick") * COARSE_DEV
    known = jnp.full((KNOWN_ROWS, HALF), -1.0, F32)
    for slot in range(COARSE_DEV):
        known = jnp.where(lane == slot, wishes[slot].astype(F32), known)
    known_ref[...] = known
    write_known(known, outs, 2 * SIDE)
    table_copy.wait()
    for copy in copies:
        copy.wait()
    for message in range(PEERS):
        pack((field, kappa), table, message, outs[message])


def links_kernel(table, field_ref, kappa_ref, source_hbm, decay_hbm, coef_ref, diagonal_ref, total_ref, source_ref, decay_ref, ext, kappa_ext, sems):
    copies = chunked_copies(((source_hbm, source_ref), (decay_hbm, decay_ref)), sems)
    for copy in copies:
        copy.start()
    fill_extended(ext, field_ref)
    fill_extended(kappa_ext, kappa_ref)

    def step(brick, carry):
        rows = brick_rows(brick)
        field = [ext[rows, lanes] for lanes in LANES]
        kappa = [kappa_ext[rows, lanes] for lanes in LANES]
        around = beside(ext, table, brick, *field)
        kappa_around = beside(kappa_ext, table, brick, *kappa)
        for half, lanes in enumerate(LANES):
            diagonal = decay_ref[rows, lanes]
            total = source_ref[rows, lanes]
            for face in range(6):
                link = 0.5 * (kappa[half] + kappa_around[face][half])
                coef_ref[face, rows, lanes] = link
                diagonal = diagonal + link
                total = total + link * around[face][half]
            diagonal_ref[rows, lanes] = diagonal
            total_ref[rows, lanes] = total
        return carry

    part = BRK // CHUNKS
    for chunk in range(CHUNKS):
        for copy in copies[2 * chunk : 2 * chunk + 2]:
            copy.wait()
        lax.fori_loop(chunk * part, (chunk + 1) * part, step, 0, unroll=UNROLL)


def first_kernel(table, diagonal_in, total_in, field_ref, known_ref, other_ref, own0, own1, own2, own3, m0, m1, m2, m3, diagonal_ref, new_ref, scale_ref, now_known_ref, l0, l1, l2, l3, o0, o1, o2, o3):
    messages, far_links = (m0, m1, m2, m3), (l0, l1, l2, l3)
    known = learned(known_ref[...], messages, 2 * SIDE, (other_ref,))
    now_known_ref[...] = known
    write_known(known, (o0, o1), SIDE)
    diagonal_ref[...] = diagonal_in[...]
    new_ref[...] = total_in[...]
    given = []
    for own, message, far_link in zip((own0, own1, own2, own3), messages, far_links):
        kappa = message[SIDE : 2 * SIDE, :]
        link = 0.5 * (own[SIDE : 2 * SIDE, :] + kappa)
        far_link[...] = link
        given.append((link * message[0:SIDE, :], 0.5 * kappa))

    def apply(rows, lanes, more):
        new_ref[rows, lanes] += more[0]
        diagonal_ref[rows, lanes] += more[1]

    from_peers(table, given, apply)

    def step(brick, carry):
        rows = brick_rows(brick)
        scale = OMEGA / diagonal_ref[rows, :]
        scale_ref[rows, :] = scale
        new_ref[rows, :] = (1.0 - OMEGA) * field_ref[rows, :] + scale * new_ref[rows, :]
        return carry

    lax.fori_loop(0, BRK, step, 0, unroll=UNROLL)
    for message, out in enumerate((o0, o1, o2, o3)):
        pack((new_ref,), table, message, out)


def sweep_kernel(table, field_ref, source_ref, coef_ref, scale_ref, new_ref, ext):
    fill_extended(ext, field_ref)

    def step(brick, carry):
        rows = brick_rows(brick)
        field = [ext[rows, lanes] for lanes in LANES]
        around = beside(ext, table, brick, *field)
        for half, lanes in enumerate(LANES):
            total = source_ref[rows, lanes]
            for face in range(6):
                total = total + coef_ref[face, rows, lanes] * around[face][half]
            new_ref[rows, lanes] = (1.0 - OMEGA) * field[half] + scale_ref[rows, lanes] * total
        return carry

    lax.fori_loop(0, BRK, step, 0, unroll=UNROLL)


def sweep_rest_kernel(table, new_in, scale_ref, known_ref, other_ref, l0, l1, l2, l3, m0, m1, m2, m3, new_ref, now_known_ref, o0, o1, o2, o3):
    messages = (m0, m1, m2, m3)
    known = learned(known_ref[...], messages, SIDE, (other_ref,))
    now_known_ref[...] = known
    write_known(known, (o0, o1), SIDE)
    new_ref[...] = new_in[...]
    given = [(link[...] * message[0:SIDE, :],) for link, message in zip((l0, l1, l2, l3), messages)]

    def apply(rows, lanes, more):
        new_ref[rows, lanes] += scale_ref[rows, lanes] * more[0]

    from_peers(table, given, apply)
    for message, out in enumerate((o0, o1, o2, o3)):
        pack((new_ref,), table, message, out)


def residual_kernel(table, field_ref, source_ref, coef_ref, diagonal_ref, left_low, left_high, field_out, ext, sem):
    copy = pltpu.make_async_copy(field_ref, field_out, sem)
    copy.start()
    fill_extended(ext, field_ref)

    def step(brick, carry):
        rows = brick_rows(brick)
        field = [ext[rows, lanes] for lanes in LANES]
        around = beside(ext, table, brick, *field)
        for half, lanes in enumerate(LANES):
            total = source_ref[rows, lanes] - diagonal_ref[rows, lanes] * field[half]
            for face in range(6):
                total = total + coef_ref[face, rows, lanes] * around[face][half]
            (left_low, left_high)[half][rows, :] = total
        return carry

    lax.fori_loop(0, BRK, step, 0, unroll=UNROLL)
    copy.wait()


def residual_rest_kernel(subs, table, low_in, high_in, known_ref, coarse_coefs, l0, l1, l2, l3, m0, m1, m2, m3, send_ref, left_low, left_high, coarse_left, held, wanted, sem):
    known = learned(known_ref[...], (m0, m1), SIDE)
    mine = known.astype(I32) - (lax.axis_index("brick") * subs + lax.axis_index("sub")) * COARSE_DEV
    mine = jnp.where((mine >= 0) & (mine < COARSE_DEV), mine + 1, 0)
    for reach in (1, 2, 4):
        mine = mine + pltpu.roll(mine, HALF - reach, 1)
    held[...] = mine
    copy = pltpu.make_async_copy(held, wanted, sem)
    copy.start()

    left_low[...] = low_in[...]
    left_high[...] = high_in[...]
    messages = (m0, m1, m2, m3)
    given = [(link[...] * message[0:SIDE, :],) for link, message in zip((l0, l1, l2, l3), messages)]

    def apply(rows, lanes, more):
        if lanes != LANES[1]:
            left_low[rows, :] += more[0][:, 0:HALF]
        if lanes != LANES[0]:
            left_high[rows, :] += more[0][:, more[0].shape[1] - HALF :]

    from_peers(table, given, apply)
    write_coarse(restricted(left_low, left_high), coarse_left, 0)
    copy.wait()
    for target in range(send_ref.shape[0]):
        chosen = jnp.maximum(wanted[0, target * COARSE_DEV] - 1, 0)
        send_ref[target, 0:SIDE, :] = coarse_left[chosen]
        send_ref[target, SIDE : 3 * SIDE, :] = coarse_coefs[chosen]


def restricted(*parts):
    rows = BRK * SIDE // 2
    paired = jnp.concatenate(
        [part[pl.ds(0, rows, stride=2), :] + part[pl.ds(1, rows, stride=2), :] for part in parts], axis=1
    )
    fine = lax.broadcasted_iota(I32, (PLANE, HALF), 0)
    target = lax.broadcasted_iota(I32, (PLANE, HALF), 1)
    same = (fine // (2 * SIDE) == target // SIDE) & ((fine % SIDE) // 2 == target % SIDE)
    table = jnp.where(same, 0.125, 0.0).astype(jnp.bfloat16)
    total = jnp.zeros((rows, HALF), F32)
    rest = paired
    for _ in range(3):
        part = rest.astype(jnp.bfloat16)
        total = total + jnp.dot(part, table, preferred_element_type=F32)
        rest = rest - part.astype(F32)
    return total


def coarse_tiles(values):
    depth = SIDE // 2
    for coarse in range(COARSE_DEV):
        cz, cy, cx = coarse // 4, coarse // 2 % 2, coarse % 2
        for pz in range(2):
            for py in range(2):
                fine = ((2 * cz + pz) * EDGE + 2 * cy + py) * EDGE + 2 * cx
                left = values[fine * depth : (fine + 1) * depth, :]
                right = values[(fine + 1) * depth : (fine + 2) * depth, :]
                yield coarse, pz, py, left + pltpu.roll(right, depth, 1)


def write_coarse(values, out_ref, base):
    for coarse, pz, py, tile in coarse_tiles(values):
        top = base + pz * (SIDE // 2)
        out_ref[coarse, top : top + SIDE // 2, py * HALF : (py + 1) * HALF] = tile


def coefficient_kernel(kappa_ref, decay_ref, out_ref, low, high):
    for ref, base in ((kappa_ref, 0), (decay_ref, SIDE)):
        low[...] = ref[:, 0:HALF]
        high[...] = ref[:, HALF:PLANE]
        write_coarse(restricted(low, high), out_ref, base)


def place_kernel(per_row, coarse_source, arrived, out_ref, sem):
    copies = [
        pltpu.make_async_copy(arrived.at[coarse_source[slot] // per_row], out_ref.at[slot], sem.at[slot])
        for slot in range(COARSE_DEV)
    ]
    for copy in copies:
        copy.start()
    for copy in copies:
        copy.wait()


def paired(block, axis, offset):
    size = lax.axis_size(axis)
    route = []
    for first in range(offset, size + offset, 2):
        one, two = first % size, (first + 1) % size
        route += [(one, two), (two, one)]
    return lax.ppermute(block, axis, route)


def shifted(block, axis, distance):
    size = lax.axis_size(axis)
    return lax.ppermute(block, axis, [(place, (place + distance) % size) for place in range(size)])


def exchanged(outgoing):
    return [
        paired(outgoing[0], "brick", 0),
        paired(outgoing[1], "brick", 1),
        paired(outgoing[2], "sub", 0),
        paired(outgoing[3], "sub", 1),
    ]


VMEM_SPEC = pl.BlockSpec(memory_space=pltpu.VMEM)
SMEM_SPEC = pl.BlockSpec(memory_space=pltpu.SMEM)
HBM_SPEC = pl.BlockSpec(memory_space=pltpu.HBM)


def in_hbm(array):
    return pltpu.with_memory_space_constraint(array, pltpu.HBM)


def in_vmem(*shape):
    return pltpu.VMEM(shape, F32)


def kernel_call(kernel, name, ins, outs, out_specs=None, scratch=()):
    return pl.pallas_call(
        kernel,
        out_shape=outs,
        in_specs=ins,
        out_specs=out_specs if out_specs is not None else tuple(VMEM_SPEC for _ in outs),
        scratch_shapes=list(scratch),
        compiler_params=pltpu.CompilerParams(vmem_limit_bytes=VMEM_LIMIT),
        name=name,
    )


def body(field_start, source, diffusion, decay_rate, neighbour, coarse_source):
    subs = lax.axis_size("sub")
    rows = BRK * SIDE
    field_start, source, diffusion, decay_rate = (
        array.reshape(rows, PLANE) for array in (field_start, source, diffusion, decay_rate)
    )
    known_shape = in_vmem(KNOWN_ROWS, HALF)
    whole = in_vmem(rows, PLANE)
    message = (in_vmem(SIDE + KNOWN_ROWS, PLANE),) * 2 + (in_vmem(SIDE, PLANE),) * 2
    double = (in_vmem(2 * SIDE + KNOWN_ROWS, PLANE),) * 2 + (in_vmem(2 * SIDE, PLANE),) * 2
    extended = pltpu.VMEM((EXT_BRICKS * SIDE, PLANE), F32)

    table, field_start, diffusion, *outgoing, known = kernel_call(
        functools.partial(start_kernel, subs),
        "route_and_pack",
        [HBM_SPEC] * 4,
        (jax.ShapeDtypeStruct((8, 128), I32),) + (whole,) * 2 + double + (known_shape,),
        out_specs=(SMEM_SPEC,) + (VMEM_SPEC,) * 7,
        scratch=[
            pltpu.VMEM((8, 128), I32),
            pltpu.SMEM((COARSE_DEV,), I32),
            pltpu.VMEM((6, BRK), I32),
            pltpu.SemaphoreType.DMA(()),
            pltpu.SemaphoreType.DMA(()),
            pltpu.SemaphoreType.DMA(()),
            pltpu.SemaphoreType.DMA((2 * CHUNKS,)),
        ],
    )(*(in_hbm(array) for array in (coarse_source, neighbour.T, field_start, diffusion)))
    own_faces = outgoing
    incoming = exchanged(outgoing)
    bricks_along = lax.axis_size("brick")
    other = shifted(known, "brick", bricks_along // 2)

    coefs, diagonal, total, source, decay_rate = kernel_call(
        links_kernel,
        "links",
        [SMEM_SPEC] + [VMEM_SPEC] * 2 + [HBM_SPEC] * 2,
        (in_vmem(6, rows, PLANE),) + (whole,) * 4,
        scratch=[extended, extended, pltpu.SemaphoreType.DMA((2 * CHUNKS,))],
    )(table, field_start, diffusion, in_hbm(source), in_hbm(decay_rate))
    coarse_coefs = kernel_call(
        coefficient_kernel, "coarse_coefficients", [VMEM_SPEC] * 2, (in_vmem(COARSE_DEV, 2 * SIDE, PLANE),),
        scratch=[pltpu.VMEM((rows, HALF), F32), pltpu.VMEM((rows, HALF), F32)],
    )(diffusion, decay_rate)[0]
    diagonal, field, scale, known, *rest = kernel_call(
        first_kernel,
        "first_sweep",
        [SMEM_SPEC] + [VMEM_SPEC] * 13,
        (whole, whole, whole, known_shape) + (in_vmem(SIDE, PLANE),) * PEERS + message,
    )(table, diagonal, total, field_start, known, other, *own_faces, *incoming)
    far_links, outgoing = rest[:PEERS], rest[PEERS:]
    incoming = exchanged(outgoing)
    other = shifted(known, "brick", bricks_along // 4)
    for _ in range(SWEEPS - 1):
        field = kernel_call(
            sweep_kernel,
            "next_sweep",
            [SMEM_SPEC] + [VMEM_SPEC] * 4,
            (whole,),
            scratch=[extended],
        )(table, field, source, coefs, scale)[0]
        field, known, *outgoing = kernel_call(
            sweep_rest_kernel,
            "next_sweep_rest",
            [SMEM_SPEC] + [VMEM_SPEC] * 12,
            (whole, known_shape) + message,
        )(table, field, scale, known, other, *far_links, *incoming)
        incoming = exchanged(outgoing)
    left = in_vmem(rows, HALF)
    left_low, left_high, field = kernel_call(
        residual_kernel,
        "residual",
        [SMEM_SPEC] + [VMEM_SPEC] * 4,
        (left, left, jax.ShapeDtypeStruct((rows, PLANE), F32)),
        out_specs=(VMEM_SPEC, VMEM_SPEC, HBM_SPEC),
        scratch=[extended, pltpu.SemaphoreType.DMA(())],
    )(table, field, source, coefs, diagonal)
    send = kernel_call(
        functools.partial(residual_rest_kernel, subs),
        "residual_rest",
        [SMEM_SPEC] + [VMEM_SPEC] * 12,
        (in_vmem(bricks_along, 3 * SIDE, PLANE),),
        scratch=[
            pltpu.VMEM((rows, HALF), F32),
            pltpu.VMEM((rows, HALF), F32),
            pltpu.VMEM((COARSE_DEV, SIDE, PLANE), F32),
            pltpu.VMEM((KNOWN_ROWS, HALF), I32),
            pltpu.SMEM((KNOWN_ROWS, HALF), I32),
            pltpu.SemaphoreType.DMA(()),
        ],
    )(table, left_low, left_high, known, coarse_coefs, *far_links, *incoming)[0]
    arrived = lax.all_to_all(send, "brick", split_axis=0, concat_axis=0, tiled=True)
    moved = kernel_call(
        functools.partial(place_kernel, subs * COARSE_DEV),
        "place",
        [SMEM_SPEC, HBM_SPEC],
        jax.ShapeDtypeStruct((COARSE_DEV, 3 * SIDE, PLANE), F32),
        out_specs=HBM_SPEC,
        scratch=[pltpu.SemaphoreType.DMA((COARSE_DEV,))],
    )(coarse_source, arrived)
    return field.reshape(BRK, SIDE, PLANE), moved.reshape(COARSE_DEV, 3, SIDE, PLANE)


def solution(mesh):
    placed = (
        P(("brick", "sub"), None, None),
        P(("brick", "sub"), None, None),
        P(("brick", "sub"), None, None),
        P(("brick", "sub"), None, None),
        P(("brick", "sub"), None),
        P(("brick", "sub")),
    )
    return jax.shard_map(
        body,
        mesh=mesh,
        in_specs=placed,
        out_specs=(P(("brick", "sub"), None, None), P(("brick", "sub"), None, None, None)),
        check_vma=False,
    )
```

```python
import functools

import jax
import jax.numpy as jnp
from jax import lax
from jax.experimental import pallas as pl
from jax.experimental.pallas import tpu as pltpu
from jax.sharding import PartitionSpec as P

EDGE = 4
LZ = 4
SWEEPS = 2
OMEGA = 0.8
UNROLL = 16

SIDE = 16
PLANE = SIDE * SIDE
HALF = PLANE // 2
DEEP = SIDE // 2
BRK = EDGE * EDGE * LZ
FACES = 6 * BRK
COARSE_DEV = BRK // 8
CAP = 16
KNOWN_ROWS = 8
CHUNKS = 4
PEERS = 4
ZERO_BRICK = BRK
EXT_BRICKS = BRK + 1
LANES = (slice(0, HALF), slice(HALF, PLANE))
SEND_ROW = 6
ODD_ROW = 7
F32 = jnp.float32
I32 = jnp.int32
VMEM_LIMIT = 16 * 1024 * 1024


def lane_iota(shape):
    return lax.broadcasted_iota(I32, shape, len(shape) - 1)


def row_iota(shape):
    return lax.broadcasted_iota(I32, shape, len(shape) - 2)


def brick_rows(index):
    return pl.ds(pl.multiple_of(index * SIDE, SIDE), SIDE)


def peers_of(subs):
    brick_at = lax.axis_index("brick")
    sub_at = lax.axis_index("sub")
    me = brick_at * subs + sub_at
    brick_step = jnp.where(brick_at % 2 == 0, subs, -subs)
    sub_step = jnp.where(sub_at % 2 == 0, 1, -1)
    return me, [me + brick_step, me - brick_step, me + sub_step, me - sub_step]


def route(subs, links_ref, table_ref, staged, bricks, sem, bricks_sem):
    me, peers = peers_of(subs)
    links_row = links_ref[...]
    eye = (row_iota((BRK, BRK)) == lane_iota((BRK, BRK))).astype(F32)

    def turned(values):
        return lax.dot_general(
            eye, values.astype(F32), (((1,), (1,)), ((), ())), preferred_element_type=F32
        ).astype(I32)

    links_col = turned(links_row >> 8) * 256 + turned(links_row & 255)

    def keyed(links, own_face):
        key = jnp.full(links.shape, -1, I32)
        floor = jnp.full(links.shape, -1, I32)
        for number, peer in enumerate(peers):
            base = peer * FACES
            there = (links >= 0) & (links >= base) & (links < base + FACES)
            order = jnp.where(peer > me, own_face, links)
            key = jnp.where(there, order + number * 65536, key)
            floor = jnp.where(there, number * 65536, floor)
        return key, floor

    key_row, _ = keyed(links_row, lane_iota((6, BRK)) * 6 + row_iota((6, BRK)))
    key_col, floor_col = keyed(links_col, row_iota((BRK, 6)) * 6 + lane_iota((BRK, 6)))

    slot_lane = lane_iota((BRK, BRK))
    brick_sub = row_iota((BRK, BRK))
    listed = jnp.zeros((BRK, BRK), F32)
    odd = jnp.zeros((BRK, 1), F32)
    for face in range(6):
        mine = key_col[:, face : face + 1]
        least = floor_col[:, face : face + 1]
        count = jnp.zeros((BRK, BRK), F32)
        for other in range(6):
            theirs = key_row[other : other + 1, :]
            count = count + ((theirs < mine) & (theirs >= least)).astype(F32)
        rank = jnp.sum(count, axis=1, keepdims=True).astype(I32)
        slot = jnp.where(mine >= 0, (least >> 16) * CAP + rank, -1)
        listed = listed + jnp.where(slot == slot_lane, (brick_sub + (face * BRK + 1)).astype(F32), 0.0)
        message = least >> 16
        if face // 2 == 0:
            plain = message < 2
        elif face // 2 == 2:
            plain = message >= 2
        else:
            plain = message < 0
        odd = odd + ((mine >= 0) & jnp.logical_not(plain)).astype(F32)
    staged[0:1, 0:BRK] = jnp.sum(listed, axis=0, keepdims=True).astype(I32) - 1
    staged[1:2, 0:BRK] = jnp.broadcast_to(jnp.sum(odd, axis=0, keepdims=True).astype(I32), (1, BRK))
    copy = pltpu.make_async_copy(staged, table_ref.at[SEND_ROW : SEND_ROW + 2], sem)
    copy.start()
    for face in range(6):
        links = links_row[face : face + 1, :]
        local = links - me * FACES
        near = (links >= 0) & (local >= 0) & (local < FACES)
        near_brick = ((local - (face ^ 1)) * 10923) >> 16
        bricks[face : face + 1, 0:BRK] = jnp.where(near, near_brick, ZERO_BRICK)
    bricks_copy = pltpu.make_async_copy(bricks, table_ref.at[0:SEND_ROW], bricks_sem)
    bricks_copy.start()
    return copy, bricks_copy


def picker(shape, lane_axis, make):
    lane = lax.broadcasted_iota(I32, shape, lane_axis)
    inner = lax.broadcasted_iota(I32, shape, 1 - lane_axis)
    return make(lane, inner).astype(F32)


def exact_dot(left, right):
    return jnp.dot(left, right, precision=lax.Precision.HIGHEST, preferred_element_type=F32)


def column_rule(place):
    return lambda lane, inner: lane == inner * SIDE + place


def lanes_rule(place):
    return lambda lane, inner: lane == place * SIDE + inner


def fold_rule(lane, inner):
    return lane % SIDE == inner


def band_mask():
    return lane_iota((SIDE, PLANE)) // SIDE == row_iota((SIDE, PLANE))


def compacted(brick, rule):
    return exact_dot(brick, picker((PLANE, SIDE), 0, rule))


def spread(compact, rule):
    return exact_dot(compact, picker((SIDE, PLANE), 1, rule))


def compact_face(ref, brick, face):
    place = (face & 1) * (SIDE - 1)
    kind = face >> 1
    cells = ref[brick_rows(brick), :]
    row = ref[pl.ds(brick * SIDE + place, 1), :]
    from_x = compacted(cells, column_rule(place))
    from_y = compacted(cells, lanes_rule(place))
    from_z = compacted(jnp.where(band_mask(), row, 0.0), fold_rule)
    return jnp.where(kind == 0, from_x, jnp.where(kind == 1, from_y, from_z))


def fits(face, message):
    return face < 2 if message < 2 else face >= 4


def pack(fields, table, message, out_ref):
    entries = [jnp.maximum(table[SEND_ROW, message * CAP + slot], 0) for slot in range(CAP)]
    if message < 2:
        column = lane_iota((SIDE, HALF)) % SIDE
        parts = [[jnp.zeros((SIDE, HALF), F32)] * 2 for _ in fields]
        for slot, entry in enumerate(entries):
            rows = brick_rows(entry & (BRK - 1))
            turn = (slot - ((entry >> 6) & 1) * (SIDE - 1)) & (HALF - 1)
            here = column == slot
            for ref, halves in zip(fields, parts):
                for half, lanes in enumerate(LANES):
                    halves[half] = jnp.where(here, pltpu.roll(ref[rows, lanes], turn, 1), halves[half])
        for number, halves in enumerate(parts):
            for half, lanes in enumerate(LANES):
                out_ref[number * SIDE : (number + 1) * SIDE, lanes] = halves[half]
    else:
        found = []
        for ref in fields:
            for entry in entries:
                row = (entry & (BRK - 1)) * SIDE + ((entry >> 6) & 1) * (SIDE - 1)
                found.append(ref[pl.ds(row, 1), :])
        for number, row in enumerate(found):
            out_ref[number : number + 1, :] = row

    for number, ref in enumerate(fields):
        pack_odd(ref, table, message, out_ref, number * SIDE)


def pack_odd(ref, table, message, out_ref, base):
    @pl.when(table[ODD_ROW, 0] > 0)
    def _():
        def step(slot, carry):
            entry = table[SEND_ROW, message * CAP + slot]
            face = entry >> 6

            @pl.when((entry >= 0) & jnp.logical_not(fits(face, message)))
            def _():
                compact = compact_face(ref, entry & (BRK - 1), face)
                if message < 2:
                    cells = spread(compact, column_rule(slot))
                    here = lane_iota((SIDE, PLANE)) % SIDE == slot
                    out_ref[base : base + SIDE, :] = jnp.where(
                        here, cells, out_ref[base : base + SIDE, :]
                    )
                else:
                    cells = jnp.where(band_mask(), spread(compact, fold_rule), 0.0)
                    here = row_iota((SIDE, PLANE)) == slot
                    out_ref[base : base + SIDE, :] = jnp.where(
                        here, jnp.sum(cells, axis=0, keepdims=True), out_ref[base : base + SIDE, :]
                    )

            return carry

        lax.fori_loop(0, CAP, step, 0)


def end_extended(ref):
    ref[BRK * SIDE : EXT_BRICKS * SIDE, :] = jnp.zeros((SIDE, PLANE), F32)


def from_peers(table, given, apply):
    column = lane_iota((SIDE, HALF)) % SIDE
    for message in range(2):
        cells = [[array[:, lanes] for lanes in LANES] for array in given[message]]
        for slot in range(CAP):
            entry = table[SEND_ROW, message * CAP + slot]
            valid = (entry >= 0) & fits(entry >> 6, message)
            entry = jnp.where(valid, entry, 0)
            place = (entry >> 6) * (SIDE - 1)
            here = column == jnp.where(valid, place, -1)
            turn = (place - slot) & (HALF - 1)
            rows = brick_rows(entry & (BRK - 1))
            for half, lanes in enumerate(LANES):
                values = [jnp.where(here, pltpu.roll(part[half], turn, 1), 0.0) for part in cells]
                apply(rows, lanes, values)
    for message in range(2, PEERS):
        for slot in range(CAP):
            entry = table[SEND_ROW, message * CAP + slot]
            valid = (entry >= 0) & fits(entry >> 6, message)
            entry = jnp.where(valid, entry, 0)
            rows = pl.ds((entry & (BRK - 1)) * SIDE + ((entry >> 6) & 1) * (SIDE - 1), 1)
            values = [jnp.where(valid, array[slot : slot + 1, :], 0.0) for array in given[message]]
            apply(rows, slice(0, PLANE), values)

    @pl.when(table[ODD_ROW, 0] > 0)
    def _():
        for message in range(PEERS):

            def step(slot, carry):
                entry = table[SEND_ROW, message * CAP + slot]
                face = entry >> 6

                @pl.when((entry >= 0) & jnp.logical_not(fits(face, message)))
                def _():
                    values = [aligned(array, message, slot, face) for array in given[message]]
                    apply(brick_rows(entry & (BRK - 1)), slice(0, PLANE), values)

                return carry

            lax.fori_loop(0, CAP, step, 0)


def aligned(cells, message, slot, face):
    if message < 2:
        compact = compacted(cells, column_rule(slot))
    else:
        row = jnp.sum(jnp.where(row_iota((SIDE, PLANE)) == slot, cells, 0.0), axis=0, keepdims=True)
        compact = compacted(jnp.where(band_mask(), row, 0.0), fold_rule)
    place = (face & 1) * (SIDE - 1)
    kind = face >> 1
    from_x = spread(compact, column_rule(place))
    from_y = spread(compact, lanes_rule(place))
    row = jnp.where(band_mask(), spread(compact, fold_rule), 0.0)
    from_z = jnp.where(
        row_iota((SIDE, PLANE)) == place, jnp.sum(row, axis=0, keepdims=True), 0.0
    )
    return jnp.where(kind == 0, from_x, jnp.where(kind == 1, from_y, from_z))


def beside(ext, table, brick, low, high):
    lane = lane_iota((SIDE, HALF))
    column = lane % SIDE
    row = row_iota((DEEP, HALF))

    def across(face):
        rows = brick_rows(table[face, brick])
        return ext[rows, 0:HALF], ext[rows, HALF:PLANE]

    def taken(cells, lanes):
        return jnp.take_along_axis(cells, lanes, axis=1)

    here = column == SIDE - 1
    lanes = jnp.where(column == 0, lane + (SIDE - 1), lane - 1)
    x_lower = [jnp.where(column == 0, pltpu.roll(far, HALF - SIDE + 1, 1), pltpu.roll(own, 1, 1)) for far, own in zip(across(0), (low, high))]
    here = column == 0
    lanes = jnp.where(column == SIDE - 1, lane - (SIDE - 1), lane + 1)
    x_upper = [jnp.where(column == SIDE - 1, pltpu.roll(far, SIDE - 1, 1), pltpu.roll(own, HALF - 1, 1)) for far, own in zip(across(1), (low, high))]
    here = lane >= HALF - SIDE
    y_lower = [
        pltpu.roll(jnp.where(here, far, own), SIDE, 1)
        for far, own in ((across(2)[1], low), (low, high))
    ]
    here = lane < SIDE
    y_upper = [
        pltpu.roll(jnp.where(here, far, own), HALF - SIDE, 1)
        for far, own in ((high, low), (across(3)[0], high))
    ]
    below = pl.ds(pl.multiple_of(table[4, brick] * SIDE + DEEP, DEEP), DEEP)
    above = pl.ds(pl.multiple_of(table[5, brick] * SIDE, DEEP), DEEP)
    last = row == DEEP - 1
    first = row == 0
    z_lower, z_upper = [], []
    for own, lanes in zip((low, high), LANES):
        top, bottom = own[0:DEEP], own[DEEP:SIDE]
        z_lower.append(pltpu.roll(jnp.concatenate([top, jnp.where(last, ext[below, lanes], bottom)], axis=0), 1, 0))
        z_upper.append(
            pltpu.roll(jnp.concatenate([jnp.where(first, ext[above, lanes], top), bottom], axis=0), SIDE - 1, 0)
        )
    return [x_lower, x_upper, y_lower, y_upper, z_lower, z_upper]


def write_known(known, outs, base):
    for out in outs[:2]:
        out[base : base + KNOWN_ROWS, 0:HALF] = known
        out[base : base + KNOWN_ROWS, HALF:PLANE] = jnp.zeros((KNOWN_ROWS, HALF), F32)


def learned(known, messages, base, others=()):
    for other in others:
        known = jnp.maximum(known, other[...])
    for message in messages[:2]:
        known = jnp.maximum(known, message[base : base + KNOWN_ROWS, 0:HALF])
    return known


def chunked_copies(pairs, sems):
    part = BRK * SIDE // CHUNKS
    copies = []
    for chunk in range(CHUNKS):
        rows = pl.ds(chunk * part, part)
        for array, target in pairs:
            copies.append(pltpu.make_async_copy(array.at[rows], target.at[rows], sems.at[len(copies)]))
    return copies


def start_kernel(subs, wishes_hbm, links_hbm, field_hbm, kappa_hbm, table, field, kappa, o0, o1, o2, o3, known_ref, staged, bricks, wishes, links, wish_sem, link_sem, table_sem, bricks_sem, sems):
    outs = (o0, o1, o2, o3)
    link_copy = pltpu.make_async_copy(links_hbm, links, link_sem)
    link_copy.start()
    wish_copy = pltpu.make_async_copy(wishes_hbm, wishes, wish_sem)
    wish_copy.start()
    copies = chunked_copies(((field_hbm, field), (kappa_hbm, kappa)), sems)
    for copy in copies:
        copy.start()
    end_extended(field)
    end_extended(kappa)
    link_copy.wait()
    table_copy, bricks_copy = route(subs, links, table, staged, bricks, table_sem, bricks_sem)
    wish_copy.wait()
    lane = lane_iota((KNOWN_ROWS, HALF)) - lax.axis_index("brick") * COARSE_DEV
    known = jnp.full((KNOWN_ROWS, HALF), -1.0, F32)
    for slot in range(COARSE_DEV):
        known = jnp.where(lane == slot, wishes[slot].astype(F32), known)
    known_ref[...] = known
    write_known(known, outs, 2 * SIDE)
    table_copy.wait()
    for copy in copies:
        copy.wait()
    for message in range(PEERS):
        pack((field, kappa), table, message, outs[message])
    bricks_copy.wait()


def links_kernel(table, ext, kappa_ext, source_hbm, decay_hbm, coef_ref, diagonal_ref, total_ref, source_ref, decay_ref, sems):
    copies = chunked_copies(((source_hbm, source_ref), (decay_hbm, decay_ref)), sems)
    for copy in copies:
        copy.start()

    def step(brick, carry):
        rows = brick_rows(brick)
        field = [ext[rows, lanes] for lanes in LANES]
        kappa = [kappa_ext[rows, lanes] for lanes in LANES]
        around = beside(ext, table, brick, *field)
        kappa_around = beside(kappa_ext, table, brick, *kappa)
        for half, lanes in enumerate(LANES):
            diagonal, total = 0.0, 0.0
            for face in range(6):
                link = 0.5 * (kappa[half] + kappa_around[face][half])
                coef_ref[face, rows, lanes] = link
                diagonal = diagonal + link
                total = total + link * around[face][half]
            diagonal_ref[rows, lanes] = diagonal
            total_ref[rows, lanes] = total
        return carry

    lax.fori_loop(0, BRK, step, 0, unroll=UNROLL)
    for copy in copies:
        copy.wait()


def first_kernel(table, diagonal_in, total_in, source_ref, decay_ref, field_ref, known_ref, other_ref, own0, own1, own2, own3, m0, m1, m2, m3, diagonal_ref, new_ref, scale_ref, now_known_ref, l0, l1, l2, l3, o0, o1, o2, o3):
    messages, far_links = (m0, m1, m2, m3), (l0, l1, l2, l3)
    known = learned(known_ref[...], messages, 2 * SIDE, (other_ref,))
    now_known_ref[...] = known
    write_known(known, (o0, o1), SIDE)
    diagonal_ref[...] = diagonal_in[...] + decay_ref[...]
    new_ref[0 : BRK * SIDE, :] = total_in[...] + source_ref[...]
    end_extended(new_ref)
    given = []
    for own, message, far_link in zip((own0, own1, own2, own3), messages, far_links):
        kappa = message[SIDE : 2 * SIDE, :]
        link = 0.5 * (own[SIDE : 2 * SIDE, :] + kappa)
        far_link[...] = link
        given.append((link * message[0:SIDE, :], 0.5 * kappa))

    def apply(rows, lanes, more):
        new_ref[rows, lanes] += more[0]
        diagonal_ref[rows, lanes] += more[1]

    from_peers(table, given, apply)

    def step(brick, carry):
        rows = brick_rows(brick)
        scale = OMEGA / diagonal_ref[rows, :]
        scale_ref[rows, :] = scale
        new_ref[rows, :] = (1.0 - OMEGA) * field_ref[rows, :] + scale * new_ref[rows, :]
        return carry

    lax.fori_loop(0, BRK, step, 0, unroll=UNROLL)
    for message, out in enumerate((o0, o1, o2, o3)):
        pack((new_ref,), table, message, out)


def sweep_kernel(table, ext, source_ref, coef_ref, scale_ref, new_ref):
    def step(brick, carry):
        rows = brick_rows(brick)
        field = [ext[rows, lanes] for lanes in LANES]
        around = beside(ext, table, brick, *field)
        for half, lanes in enumerate(LANES):
            total = source_ref[rows, lanes]
            for face in range(6):
                total = total + coef_ref[face, rows, lanes] * around[face][half]
            new_ref[rows, lanes] = (1.0 - OMEGA) * field[half] + scale_ref[rows, lanes] * total
        return carry

    lax.fori_loop(0, BRK, step, 0, unroll=UNROLL)


def sweep_rest_kernel(table, new_in, scale_ref, known_ref, other_ref, l0, l1, l2, l3, m0, m1, m2, m3, new_ref, now_known_ref, o0, o1, o2, o3):
    messages = (m0, m1, m2, m3)
    known = learned(known_ref[...], messages, SIDE, (other_ref,))
    now_known_ref[...] = known
    write_known(known, (o0, o1), SIDE)
    new_ref[0 : BRK * SIDE, :] = new_in[...]
    end_extended(new_ref)
    given = [(link[...] * message[0:SIDE, :],) for link, message in zip((l0, l1, l2, l3), messages)]

    def apply(rows, lanes, more):
        new_ref[rows, lanes] += scale_ref[rows, lanes] * more[0]

    from_peers(table, given, apply)
    for message, out in enumerate((o0, o1, o2, o3)):
        pack((new_ref,), table, message, out)


def residual_kernel(table, ext, source_ref, coef_ref, diagonal_ref, left_low, left_high, field_out, sem):
    copy = pltpu.make_async_copy(ext.at[0 : BRK * SIDE], field_out, sem)
    copy.start()

    def step(brick, carry):
        rows = brick_rows(brick)
        field = [ext[rows, lanes] for lanes in LANES]
        around = beside(ext, table, brick, *field)
        for half, lanes in enumerate(LANES):
            total = source_ref[rows, lanes] - diagonal_ref[rows, lanes] * field[half]
            for face in range(6):
                total = total + coef_ref[face, rows, lanes] * around[face][half]
            (left_low, left_high)[half][rows, :] = total
        return carry

    lax.fori_loop(0, BRK, step, 0, unroll=UNROLL)
    copy.wait()


def residual_rest_kernel(subs, table, low_in, high_in, known_ref, coarse_coefs, l0, l1, l2, l3, m0, m1, m2, m3, send_ref, left_low, left_high, coarse_left, held, wanted, sem):
    known = learned(known_ref[...], (m0, m1), SIDE)
    mine = known.astype(I32) - (lax.axis_index("brick") * subs + lax.axis_index("sub")) * COARSE_DEV
    mine = jnp.where((mine >= 0) & (mine < COARSE_DEV), mine + 1, 0)
    for reach in (1, 2, 4):
        mine = mine + pltpu.roll(mine, HALF - reach, 1)
    held[...] = mine
    copy = pltpu.make_async_copy(held, wanted, sem)
    copy.start()

    left_low[...] = low_in[...]
    left_high[...] = high_in[...]
    messages = (m0, m1, m2, m3)
    given = [(link[...] * message[0:SIDE, :],) for link, message in zip((l0, l1, l2, l3), messages)]

    def apply(rows, lanes, more):
        if lanes != LANES[1]:
            left_low[rows, :] += more[0][:, 0:HALF]
        if lanes != LANES[0]:
            left_high[rows, :] += more[0][:, more[0].shape[1] - HALF :]

    from_peers(table, given, apply)
    write_coarse(restricted(left_low, left_high), coarse_left, 0)
    copy.wait()
    for target in range(send_ref.shape[0]):
        chosen = jnp.maximum(wanted[0, target * COARSE_DEV] - 1, 0)
        send_ref[target, 0:SIDE, :] = coarse_left[chosen]
        send_ref[target, SIDE : 3 * SIDE, :] = coarse_coefs[chosen]


def restricted(*parts):
    rows = BRK * SIDE // 2
    paired = jnp.concatenate(
        [part[pl.ds(0, rows, stride=2), :] + part[pl.ds(1, rows, stride=2), :] for part in parts], axis=1
    )
    fine = lax.broadcasted_iota(I32, (PLANE, HALF), 0)
    target = lax.broadcasted_iota(I32, (PLANE, HALF), 1)
    same = (fine // (2 * SIDE) == target // SIDE) & ((fine % SIDE) // 2 == target % SIDE)
    table = jnp.where(same, 0.125, 0.0).astype(jnp.bfloat16)
    total = jnp.zeros((rows, HALF), F32)
    rest = paired
    for _ in range(3):
        part = rest.astype(jnp.bfloat16)
        total = total + jnp.dot(part, table, preferred_element_type=F32)
        rest = rest - part.astype(F32)
    return total


def coarse_tiles(values):
    depth = SIDE // 2
    for coarse in range(COARSE_DEV):
        cz, cy, cx = coarse // 4, coarse // 2 % 2, coarse % 2
        for pz in range(2):
            for py in range(2):
                fine = ((2 * cz + pz) * EDGE + 2 * cy + py) * EDGE + 2 * cx
                left = values[fine * depth : (fine + 1) * depth, :]
                right = values[(fine + 1) * depth : (fine + 2) * depth, :]
                yield coarse, pz, py, left + pltpu.roll(right, depth, 1)


def write_coarse(values, out_ref, base):
    for coarse, pz, py, tile in coarse_tiles(values):
        top = base + pz * (SIDE // 2)
        out_ref[coarse, top : top + SIDE // 2, py * HALF : (py + 1) * HALF] = tile


def coefficient_kernel(kappa_ref, decay_ref, out_ref, low, high):
    for ref, base in ((kappa_ref, 0), (decay_ref, SIDE)):
        low[...] = ref[0 : BRK * SIDE, 0:HALF]
        high[...] = ref[0 : BRK * SIDE, HALF:PLANE]
        write_coarse(restricted(low, high), out_ref, base)


def place_kernel(per_row, coarse_source, arrived, out_ref, sem):
    copies = [
        pltpu.make_async_copy(arrived.at[coarse_source[slot] // per_row], out_ref.at[slot], sem.at[slot])
        for slot in range(COARSE_DEV)
    ]
    for copy in copies:
        copy.start()
    for copy in copies:
        copy.wait()


def paired(block, axis, offset):
    size = lax.axis_size(axis)
    route = []
    for first in range(offset, size + offset, 2):
        one, two = first % size, (first + 1) % size
        route += [(one, two), (two, one)]
    return lax.ppermute(block, axis, route)


def shifted(block, axis, distance):
    size = lax.axis_size(axis)
    return lax.ppermute(block, axis, [(place, (place + distance) % size) for place in range(size)])


def exchanged(outgoing):
    return [
        paired(outgoing[0], "brick", 0),
        paired(outgoing[1], "brick", 1),
        paired(outgoing[2], "sub", 0),
        paired(outgoing[3], "sub", 1),
    ]


VMEM_SPEC = pl.BlockSpec(memory_space=pltpu.VMEM)
SMEM_SPEC = pl.BlockSpec(memory_space=pltpu.SMEM)
HBM_SPEC = pl.BlockSpec(memory_space=pltpu.HBM)


def in_hbm(array):
    return pltpu.with_memory_space_constraint(array, pltpu.HBM)


def in_vmem(*shape):
    return pltpu.VMEM(shape, F32)


def kernel_call(kernel, name, ins, outs, out_specs=None, scratch=()):
    return pl.pallas_call(
        kernel,
        out_shape=outs,
        in_specs=ins,
        out_specs=out_specs if out_specs is not None else tuple(VMEM_SPEC for _ in outs),
        scratch_shapes=list(scratch),
        compiler_params=pltpu.CompilerParams(vmem_limit_bytes=VMEM_LIMIT),
        name=name,
    )


def body(field_start, source, diffusion, decay_rate, neighbour, coarse_source):
    subs = lax.axis_size("sub")
    rows = BRK * SIDE
    field_start, source, diffusion, decay_rate = (
        array.reshape(rows, PLANE) for array in (field_start, source, diffusion, decay_rate)
    )
    known_shape = in_vmem(KNOWN_ROWS, HALF)
    whole = in_vmem(rows, PLANE)
    extended = in_vmem(EXT_BRICKS * SIDE, PLANE)
    message = (in_vmem(SIDE + KNOWN_ROWS, PLANE),) * 2 + (in_vmem(SIDE, PLANE),) * 2
    double = (in_vmem(2 * SIDE + KNOWN_ROWS, PLANE),) * 2 + (in_vmem(2 * SIDE, PLANE),) * 2

    table, field_start, diffusion, *outgoing, known = kernel_call(
        functools.partial(start_kernel, subs),
        "route_and_pack",
        [HBM_SPEC] * 4,
        (jax.ShapeDtypeStruct((8, 128), I32),) + (extended,) * 2 + double + (known_shape,),
        out_specs=(SMEM_SPEC,) + (VMEM_SPEC,) * 7,
        scratch=[
            pltpu.VMEM((2, HALF), I32),
            pltpu.VMEM((SEND_ROW, HALF), I32),
            pltpu.SMEM((COARSE_DEV,), I32),
            pltpu.VMEM((6, BRK), I32),
            pltpu.SemaphoreType.DMA(()),
            pltpu.SemaphoreType.DMA(()),
            pltpu.SemaphoreType.DMA(()),
            pltpu.SemaphoreType.DMA(()),
            pltpu.SemaphoreType.DMA((2 * CHUNKS,)),
        ],
    )(*(in_hbm(array) for array in (coarse_source, neighbour.T, field_start, diffusion)))
    own_faces = outgoing
    incoming = exchanged(outgoing)
    bricks_along = lax.axis_size("brick")
    other = shifted(known, "brick", bricks_along // 2)

    coefs, diagonal, total, source, decay_rate = kernel_call(
        links_kernel,
        "links",
        [SMEM_SPEC] + [VMEM_SPEC] * 2 + [HBM_SPEC] * 2,
        (in_vmem(6, rows, PLANE),) + (whole,) * 4,
        scratch=[pltpu.SemaphoreType.DMA((2 * CHUNKS,))],
    )(table, field_start, diffusion, in_hbm(source), in_hbm(decay_rate))
    coarse_coefs = kernel_call(
        coefficient_kernel, "coarse_coefficients", [VMEM_SPEC] * 2, (in_vmem(COARSE_DEV, 2 * SIDE, PLANE),),
        scratch=[pltpu.VMEM((rows, HALF), F32), pltpu.VMEM((rows, HALF), F32)],
    )(diffusion, decay_rate)[0]
    diagonal, field, scale, known, *rest = kernel_call(
        first_kernel,
        "first_sweep",
        [SMEM_SPEC] + [VMEM_SPEC] * 15,
        (whole, extended, whole, known_shape) + (in_vmem(SIDE, PLANE),) * PEERS + message,
    )(table, diagonal, total, source, decay_rate, field_start, known, other, *own_faces, *incoming)
    far_links, outgoing = rest[:PEERS], rest[PEERS:]
    incoming = exchanged(outgoing)
    other = shifted(known, "brick", bricks_along // 4)
    for _ in range(SWEEPS - 1):
        field = kernel_call(
            sweep_kernel,
            "next_sweep",
            [SMEM_SPEC] + [VMEM_SPEC] * 4,
            (whole,),
        )(table, field, source, coefs, scale)[0]
        field, known, *outgoing = kernel_call(
            sweep_rest_kernel,
            "next_sweep_rest",
            [SMEM_SPEC] + [VMEM_SPEC] * 12,
            (extended, known_shape) + message,
        )(table, field, scale, known, other, *far_links, *incoming)
        incoming = exchanged(outgoing)
    left = in_vmem(rows, HALF)
    left_low, left_high, field = kernel_call(
        residual_kernel,
        "residual",
        [SMEM_SPEC] + [VMEM_SPEC] * 4,
        (left, left, jax.ShapeDtypeStruct((rows, PLANE), F32)),
        out_specs=(VMEM_SPEC, VMEM_SPEC, HBM_SPEC),
        scratch=[pltpu.SemaphoreType.DMA(())],
    )(table, field, source, coefs, diagonal)
    send = kernel_call(
        functools.partial(residual_rest_kernel, subs),
        "residual_rest",
        [SMEM_SPEC] + [VMEM_SPEC] * 12,
        (in_vmem(bricks_along, 3 * SIDE, PLANE),),
        scratch=[
            pltpu.VMEM((rows, HALF), F32),
            pltpu.VMEM((rows, HALF), F32),
            pltpu.VMEM((COARSE_DEV, SIDE, PLANE), F32),
            pltpu.VMEM((KNOWN_ROWS, HALF), I32),
            pltpu.SMEM((KNOWN_ROWS, HALF), I32),
            pltpu.SemaphoreType.DMA(()),
        ],
    )(table, left_low, left_high, known, coarse_coefs, *far_links, *incoming)[0]
    arrived = lax.all_to_all(send, "brick", split_axis=0, concat_axis=0, tiled=True)
    moved = kernel_call(
        functools.partial(place_kernel, subs * COARSE_DEV),
        "place",
        [SMEM_SPEC, HBM_SPEC],
        jax.ShapeDtypeStruct((COARSE_DEV, 3 * SIDE, PLANE), F32),
        out_specs=HBM_SPEC,
        scratch=[pltpu.SemaphoreType.DMA((COARSE_DEV,))],
    )(coarse_source, arrived)
    return field.reshape(BRK, SIDE, PLANE), moved.reshape(COARSE_DEV, 3, SIDE, PLANE)


def solution(mesh):
    placed = (
        P(("brick", "sub"), None, None),
        P(("brick", "sub"), None, None),
        P(("brick", "sub"), None, None),
        P(("brick", "sub"), None, None),
        P(("brick", "sub"), None),
        P(("brick", "sub")),
    )
    return jax.shard_map(
        body,
        mesh=mesh,
        in_specs=placed,
        out_specs=(P(("brick", "sub"), None, None), P(("brick", "sub"), None, None, None)),
        check_vma=False,
    )
```

```python
import functools

import jax
import jax.numpy as jnp
from jax import lax
from jax.experimental import pallas as pl
from jax.experimental.pallas import tpu as pltpu
from jax.sharding import PartitionSpec as P

EDGE = 4
LZ = 4
SWEEPS = 2
OMEGA = 0.8
UNROLL = 16

SIDE = 16
PLANE = SIDE * SIDE
HALF = PLANE // 2
DEEP = SIDE // 2
BRK = EDGE * EDGE * LZ
FACES = 6 * BRK
COARSE_DEV = BRK // 8
CAP = 16
KNOWN_ROWS = 8
CHUNKS = 4
PEERS = 4
ZERO_BRICK = BRK
EXT_BRICKS = BRK + 1
LANES = (slice(0, HALF), slice(HALF, PLANE))
SEND_ROW = 6
ODD_ROW = 7
F32 = jnp.float32
I32 = jnp.int32
VMEM_LIMIT = 16 * 1024 * 1024


def lane_iota(shape):
    return lax.broadcasted_iota(I32, shape, len(shape) - 1)


def row_iota(shape):
    return lax.broadcasted_iota(I32, shape, len(shape) - 2)


def brick_rows(index):
    return pl.ds(pl.multiple_of(index * SIDE, SIDE), SIDE)


def peers_of(subs):
    brick_at = lax.axis_index("brick")
    sub_at = lax.axis_index("sub")
    me = brick_at * subs + sub_at
    brick_step = jnp.where(brick_at % 2 == 0, subs, -subs)
    sub_step = jnp.where(sub_at % 2 == 0, 1, -1)
    return me, [me + brick_step, me - brick_step, me + sub_step, me - sub_step]


def route(subs, links_ref, table_ref, staged, bricks, sem, bricks_sem):
    me, peers = peers_of(subs)
    links_row = links_ref[...]
    eye = (row_iota((BRK, BRK)) == lane_iota((BRK, BRK))).astype(F32)

    def turned(values):
        return lax.dot_general(
            eye, values.astype(F32), (((1,), (1,)), ((), ())), preferred_element_type=F32
        ).astype(I32)

    links_col = turned(links_row >> 8) * 256 + turned(links_row & 255)

    def keyed(links, own_face):
        key = jnp.full(links.shape, -1, I32)
        floor = jnp.full(links.shape, -1, I32)
        for number, peer in enumerate(peers):
            base = peer * FACES
            there = (links >= 0) & (links >= base) & (links < base + FACES)
            order = jnp.where(peer > me, own_face, links)
            key = jnp.where(there, order + number * 65536, key)
            floor = jnp.where(there, number * 65536, floor)
        return key, floor

    key_row, _ = keyed(links_row, lane_iota((6, BRK)) * 6 + row_iota((6, BRK)))
    key_col, floor_col = keyed(links_col, row_iota((BRK, 6)) * 6 + lane_iota((BRK, 6)))

    slot_lane = lane_iota((BRK, BRK))
    brick_sub = row_iota((BRK, BRK))
    listed = jnp.zeros((BRK, BRK), F32)
    odd = jnp.zeros((BRK, 1), F32)
    for face in range(6):
        mine = key_col[:, face : face + 1]
        least = floor_col[:, face : face + 1]
        count = jnp.zeros((BRK, BRK), F32)
        for other in range(6):
            theirs = key_row[other : other + 1, :]
            count = count + ((theirs < mine) & (theirs >= least)).astype(F32)
        rank = jnp.sum(count, axis=1, keepdims=True).astype(I32)
        slot = jnp.where(mine >= 0, (least >> 16) * CAP + rank, -1)
        listed = listed + jnp.where(slot == slot_lane, (brick_sub + (face * BRK + 1)).astype(F32), 0.0)
        message = least >> 16
        if face // 2 == 0:
            plain = message < 2
        elif face // 2 == 2:
            plain = message >= 2
        else:
            plain = message < 0
        odd = odd + ((mine >= 0) & jnp.logical_not(plain)).astype(F32)
    staged[0:1, 0:BRK] = jnp.sum(listed, axis=0, keepdims=True).astype(I32) - 1
    staged[1:2, 0:BRK] = jnp.broadcast_to(jnp.sum(odd, axis=0, keepdims=True).astype(I32), (1, BRK))
    copy = pltpu.make_async_copy(staged, table_ref.at[SEND_ROW : SEND_ROW + 2], sem)
    copy.start()
    for face in range(6):
        links = links_row[face : face + 1, :]
        local = links - me * FACES
        near = (links >= 0) & (local >= 0) & (local < FACES)
        near_brick = ((local - (face ^ 1)) * 10923) >> 16
        bricks[face : face + 1, 0:BRK] = jnp.where(near, near_brick, ZERO_BRICK)
    bricks_copy = pltpu.make_async_copy(bricks, table_ref.at[0:SEND_ROW], bricks_sem)
    bricks_copy.start()
    return copy, bricks_copy


def picker(shape, lane_axis, make):
    lane = lax.broadcasted_iota(I32, shape, lane_axis)
    inner = lax.broadcasted_iota(I32, shape, 1 - lane_axis)
    return make(lane, inner).astype(F32)


def exact_dot(left, right):
    return jnp.dot(left, right, precision=lax.Precision.HIGHEST, preferred_element_type=F32)


def column_rule(place):
    return lambda lane, inner: lane == inner * SIDE + place


def lanes_rule(place):
    return lambda lane, inner: lane == place * SIDE + inner


def fold_rule(lane, inner):
    return lane % SIDE == inner


def band_mask():
    return lane_iota((SIDE, PLANE)) // SIDE == row_iota((SIDE, PLANE))


def compacted(brick, rule):
    return exact_dot(brick, picker((PLANE, SIDE), 0, rule))


def spread(compact, rule):
    return exact_dot(compact, picker((SIDE, PLANE), 1, rule))


def compact_face(ref, brick, face):
    place = (face & 1) * (SIDE - 1)
    kind = face >> 1
    cells = ref[brick_rows(brick), :]
    row = ref[pl.ds(brick * SIDE + place, 1), :]
    from_x = compacted(cells, column_rule(place))
    from_y = compacted(cells, lanes_rule(place))
    from_z = compacted(jnp.where(band_mask(), row, 0.0), fold_rule)
    return jnp.where(kind == 0, from_x, jnp.where(kind == 1, from_y, from_z))


def fits(face, message):
    return face < 2 if message < 2 else face >= 4


def pack(fields, table, message, out_ref):
    entries = [jnp.maximum(table[SEND_ROW, message * CAP + slot], 0) for slot in range(CAP)]
    if message < 2:
        column = lane_iota((SIDE, HALF)) % SIDE
        parts = [[jnp.zeros((SIDE, HALF), F32)] * 2 for _ in fields]
        for slot, entry in enumerate(entries):
            rows = brick_rows(entry & (BRK - 1))
            turn = (slot - ((entry >> 6) & 1) * (SIDE - 1)) & (HALF - 1)
            here = column == slot
            for ref, halves in zip(fields, parts):
                for half, lanes in enumerate(LANES):
                    halves[half] = jnp.where(here, pltpu.roll(ref[rows, lanes], turn, 1), halves[half])
        for number, halves in enumerate(parts):
            for half, lanes in enumerate(LANES):
                out_ref[number * SIDE : (number + 1) * SIDE, lanes] = halves[half]
    else:
        found = []
        for ref in fields:
            for entry in entries:
                row = (entry & (BRK - 1)) * SIDE + ((entry >> 6) & 1) * (SIDE - 1)
                found.append(ref[pl.ds(row, 1), :])
        for number, row in enumerate(found):
            out_ref[number : number + 1, :] = row

    for number, ref in enumerate(fields):
        pack_odd(ref, table, message, out_ref, number * SIDE)


def pack_odd(ref, table, message, out_ref, base):
    @pl.when(table[ODD_ROW, 0] > 0)
    def _():
        def step(slot, carry):
            entry = table[SEND_ROW, message * CAP + slot]
            face = entry >> 6

            @pl.when((entry >= 0) & jnp.logical_not(fits(face, message)))
            def _():
                compact = compact_face(ref, entry & (BRK - 1), face)
                if message < 2:
                    cells = spread(compact, column_rule(slot))
                    here = lane_iota((SIDE, PLANE)) % SIDE == slot
                    out_ref[base : base + SIDE, :] = jnp.where(
                        here, cells, out_ref[base : base + SIDE, :]
                    )
                else:
                    cells = jnp.where(band_mask(), spread(compact, fold_rule), 0.0)
                    here = row_iota((SIDE, PLANE)) == slot
                    out_ref[base : base + SIDE, :] = jnp.where(
                        here, jnp.sum(cells, axis=0, keepdims=True), out_ref[base : base + SIDE, :]
                    )

            return carry

        lax.fori_loop(0, CAP, step, 0)


def end_extended(ref):
    ref[BRK * SIDE : EXT_BRICKS * SIDE, :] = jnp.zeros((SIDE, PLANE), F32)


def from_peers(table, given, apply):
    column = lane_iota((SIDE, HALF)) % SIDE
    for message in range(2):
        cells = [[array[:, lanes] for lanes in LANES] for array in given[message]]
        for slot in range(CAP):
            entry = table[SEND_ROW, message * CAP + slot]
            valid = (entry >= 0) & fits(entry >> 6, message)
            entry = jnp.where(valid, entry, 0)
            place = (entry >> 6) * (SIDE - 1)
            here = column == jnp.where(valid, place, -1)
            turn = (place - slot) & (HALF - 1)
            rows = brick_rows(entry & (BRK - 1))
            for half, lanes in enumerate(LANES):
                values = [jnp.where(here, pltpu.roll(part[half], turn, 1), 0.0) for part in cells]
                apply(rows, lanes, values)
    for message in range(2, PEERS):
        for slot in range(CAP):
            entry = table[SEND_ROW, message * CAP + slot]
            valid = (entry >= 0) & fits(entry >> 6, message)
            entry = jnp.where(valid, entry, 0)
            rows = pl.ds((entry & (BRK - 1)) * SIDE + ((entry >> 6) & 1) * (SIDE - 1), 1)
            values = [jnp.where(valid, array[slot : slot + 1, :], 0.0) for array in given[message]]
            apply(rows, slice(0, PLANE), values)

    @pl.when(table[ODD_ROW, 0] > 0)
    def _():
        for message in range(PEERS):

            def step(slot, carry):
                entry = table[SEND_ROW, message * CAP + slot]
                face = entry >> 6

                @pl.when((entry >= 0) & jnp.logical_not(fits(face, message)))
                def _():
                    values = [aligned(array, message, slot, face) for array in given[message]]
                    apply(brick_rows(entry & (BRK - 1)), slice(0, PLANE), values)

                return carry

            lax.fori_loop(0, CAP, step, 0)


def aligned(cells, message, slot, face):
    if message < 2:
        compact = compacted(cells, column_rule(slot))
    else:
        row = jnp.sum(jnp.where(row_iota((SIDE, PLANE)) == slot, cells, 0.0), axis=0, keepdims=True)
        compact = compacted(jnp.where(band_mask(), row, 0.0), fold_rule)
    place = (face & 1) * (SIDE - 1)
    kind = face >> 1
    from_x = spread(compact, column_rule(place))
    from_y = spread(compact, lanes_rule(place))
    row = jnp.where(band_mask(), spread(compact, fold_rule), 0.0)
    from_z = jnp.where(
        row_iota((SIDE, PLANE)) == place, jnp.sum(row, axis=0, keepdims=True), 0.0
    )
    return jnp.where(kind == 0, from_x, jnp.where(kind == 1, from_y, from_z))


def beside(ext, table, brick, low, high):
    lane = lane_iota((SIDE, HALF))
    column = lane % SIDE
    row = row_iota((DEEP, HALF))

    def across(face):
        rows = brick_rows(table[face, brick])
        return ext[rows, 0:HALF], ext[rows, HALF:PLANE]

    def taken(cells, lanes):
        return jnp.take_along_axis(cells, lanes, axis=1)

    here = column == SIDE - 1
    lanes = jnp.where(column == 0, lane + (SIDE - 1), lane - 1)
    x_lower = [jnp.where(column == 0, pltpu.roll(far, HALF - SIDE + 1, 1), pltpu.roll(own, 1, 1)) for far, own in zip(across(0), (low, high))]
    here = column == 0
    lanes = jnp.where(column == SIDE - 1, lane - (SIDE - 1), lane + 1)
    x_upper = [jnp.where(column == SIDE - 1, pltpu.roll(far, SIDE - 1, 1), pltpu.roll(own, HALF - 1, 1)) for far, own in zip(across(1), (low, high))]
    here = lane >= HALF - SIDE
    y_lower = [
        pltpu.roll(jnp.where(here, far, own), SIDE, 1)
        for far, own in ((across(2)[1], low), (low, high))
    ]
    here = lane < SIDE
    y_upper = [
        pltpu.roll(jnp.where(here, far, own), HALF - SIDE, 1)
        for far, own in ((high, low), (across(3)[0], high))
    ]
    below = pl.ds(pl.multiple_of(table[4, brick] * SIDE + DEEP, DEEP), DEEP)
    above = pl.ds(pl.multiple_of(table[5, brick] * SIDE, DEEP), DEEP)
    last = row == DEEP - 1
    first = row == 0
    z_lower, z_upper = [], []
    for own, lanes in zip((low, high), LANES):
        top, bottom = own[0:DEEP], own[DEEP:SIDE]
        z_lower.append(pltpu.roll(jnp.concatenate([top, jnp.where(last, ext[below, lanes], bottom)], axis=0), 1, 0))
        z_upper.append(
            pltpu.roll(jnp.concatenate([jnp.where(first, ext[above, lanes], top), bottom], axis=0), SIDE - 1, 0)
        )
    return [x_lower, x_upper, y_lower, y_upper, z_lower, z_upper]


def write_known(known, outs, base):
    for out in outs[:2]:
        out[base : base + KNOWN_ROWS, 0:HALF] = known
        out[base : base + KNOWN_ROWS, HALF:PLANE] = jnp.zeros((KNOWN_ROWS, HALF), F32)


def learned(known, messages, base, others=()):
    for other in others:
        known = jnp.maximum(known, other[...])
    for message in messages[:2]:
        known = jnp.maximum(known, message[base : base + KNOWN_ROWS, 0:HALF])
    return known


def chunked_copies(pairs, sems):
    part = BRK * SIDE // CHUNKS
    copies = []
    for chunk in range(CHUNKS):
        rows = pl.ds(chunk * part, part)
        for array, target in pairs:
            copies.append(pltpu.make_async_copy(array.at[rows], target.at[rows], sems.at[len(copies)]))
    return copies


def start_kernel(subs, wishes_hbm, links_hbm, field_hbm, kappa_hbm, table, field, kappa, o0, o1, o2, o3, known_ref, staged, bricks, wishes, links, wish_sem, link_sem, table_sem, bricks_sem, sems):
    outs = (o0, o1, o2, o3)
    link_copy = pltpu.make_async_copy(links_hbm, links, link_sem)
    link_copy.start()
    wish_copy = pltpu.make_async_copy(wishes_hbm, wishes, wish_sem)
    wish_copy.start()
    copies = chunked_copies(((field_hbm, field), (kappa_hbm, kappa)), sems)
    for copy in copies:
        copy.start()
    end_extended(field)
    end_extended(kappa)
    link_copy.wait()
    table_copy, bricks_copy = route(subs, links, table, staged, bricks, table_sem, bricks_sem)
    wish_copy.wait()
    lane = lane_iota((KNOWN_ROWS, HALF)) - lax.axis_index("brick") * COARSE_DEV
    known = jnp.full((KNOWN_ROWS, HALF), -1.0, F32)
    for slot in range(COARSE_DEV):
        known = jnp.where(lane == slot, wishes[slot].astype(F32), known)
    known_ref[...] = known
    write_known(known, outs, 2 * SIDE)
    table_copy.wait()
    for copy in copies:
        copy.wait()
    for message in range(PEERS):
        pack((field, kappa), table, message, outs[message])
    bricks_copy.wait()


def links_kernel(table, ext, kappa_ext, source_hbm, decay_hbm, coef_ref, diagonal_ref, total_ref, source_ref, decay_ref, sems):
    copies = chunked_copies(((source_hbm, source_ref), (decay_hbm, decay_ref)), sems)
    for copy in copies:
        copy.start()

    def step(brick, carry):
        rows = brick_rows(brick)
        field = [ext[rows, lanes] for lanes in LANES]
        kappa = [kappa_ext[rows, lanes] for lanes in LANES]
        around = beside(ext, table, brick, *field)
        kappa_around = beside(kappa_ext, table, brick, *kappa)
        for half, lanes in enumerate(LANES):
            diagonal, total = 0.0, 0.0
            for face in range(6):
                link = 0.5 * (kappa[half] + kappa_around[face][half])
                coef_ref[face, rows, lanes] = link
                diagonal = diagonal + link
                total = total + link * around[face][half]
            diagonal_ref[rows, lanes] = diagonal
            total_ref[rows, lanes] = total
        return carry

    lax.fori_loop(0, BRK, step, 0, unroll=UNROLL)
    for copy in copies:
        copy.wait()


def first_kernel(table, diagonal_in, total_in, source_ref, decay_ref, field_ref, known_ref, other_ref, own0, own1, own2, own3, m0, m1, m2, m3, diagonal_ref, new_ref, scale_ref, now_known_ref, l0, l1, l2, l3, o0, o1, o2, o3):
    messages, far_links = (m0, m1, m2, m3), (l0, l1, l2, l3)
    known = learned(known_ref[...], messages, 2 * SIDE, (other_ref,))
    now_known_ref[...] = known
    write_known(known, (o0, o1), SIDE)
    diagonal_ref[...] = diagonal_in[...] + decay_ref[...]
    new_ref[0 : BRK * SIDE, :] = total_in[...] + source_ref[...]
    end_extended(new_ref)
    given = []
    for own, message, far_link in zip((own0, own1, own2, own3), messages, far_links):
        kappa = message[SIDE : 2 * SIDE, :]
        link = 0.5 * (own[SIDE : 2 * SIDE, :] + kappa)
        far_link[...] = link
        given.append((link * message[0:SIDE, :], 0.5 * kappa))

    def apply(rows, lanes, more):
        new_ref[rows, lanes] += more[0]
        diagonal_ref[rows, lanes] += more[1]

    from_peers(table, given, apply)

    def step(brick, carry):
        rows = brick_rows(brick)
        scale = OMEGA / diagonal_ref[rows, :]
        scale_ref[rows, :] = scale
        new_ref[rows, :] = (1.0 - OMEGA) * field_ref[rows, :] + scale * new_ref[rows, :]
        return carry

    lax.fori_loop(0, BRK, step, 0, unroll=UNROLL)
    for message, out in enumerate((o0, o1, o2, o3)):
        pack((new_ref,), table, message, out)


def sweep_kernel(table, ext, source_ref, coef_ref, scale_ref, new_ref):
    def step(brick, carry):
        rows = brick_rows(brick)
        field = [ext[rows, lanes] for lanes in LANES]
        around = beside(ext, table, brick, *field)
        for half, lanes in enumerate(LANES):
            total = source_ref[rows, lanes]
            for face in range(6):
                total = total + coef_ref[face, rows, lanes] * around[face][half]
            new_ref[rows, lanes] = (1.0 - OMEGA) * field[half] + scale_ref[rows, lanes] * total
        return carry

    lax.fori_loop(0, BRK, step, 0, unroll=UNROLL)


def sweep_rest_kernel(table, new_in, scale_ref, known_ref, other_ref, l0, l1, l2, l3, m0, m1, m2, m3, new_ref, now_known_ref, o0, o1, o2, o3):
    messages = (m0, m1, m2, m3)
    known = learned(known_ref[...], messages, SIDE, (other_ref,))
    now_known_ref[...] = known
    write_known(known, (o0, o1), SIDE)
    new_ref[0 : BRK * SIDE, :] = new_in[...]
    end_extended(new_ref)
    given = [(link[...] * message[0:SIDE, :],) for link, message in zip((l0, l1, l2, l3), messages)]

    def apply(rows, lanes, more):
        new_ref[rows, lanes] += scale_ref[rows, lanes] * more[0]

    from_peers(table, given, apply)
    for message, out in enumerate((o0, o1, o2, o3)):
        pack((new_ref,), table, message, out)


def residual_kernel(table, ext, source_ref, coef_ref, diagonal_ref, left_low, left_high, field_out, sem):
    copy = pltpu.make_async_copy(ext.at[0 : BRK * SIDE], field_out, sem)
    copy.start()

    def step(brick, carry):
        rows = brick_rows(brick)
        field = [ext[rows, lanes] for lanes in LANES]
        around = beside(ext, table, brick, *field)
        for half, lanes in enumerate(LANES):
            total = source_ref[rows, lanes] - diagonal_ref[rows, lanes] * field[half]
            for face in range(6):
                total = total + coef_ref[face, rows, lanes] * around[face][half]
            (left_low, left_high)[half][rows, :] = total
        return carry

    lax.fori_loop(0, BRK, step, 0, unroll=UNROLL)
    copy.wait()


def residual_rest_kernel(subs, table, low_in, high_in, known_ref, coarse_coefs, l0, l1, l2, l3, m0, m1, m2, m3, send_ref, left_low, left_high, coarse_left, held, wanted, sem):
    known = learned(known_ref[...], (m0, m1), SIDE)
    mine = known.astype(I32) - (lax.axis_index("brick") * subs + lax.axis_index("sub")) * COARSE_DEV
    mine = jnp.where((mine >= 0) & (mine < COARSE_DEV), mine + 1, 0)
    for reach in (1, 2, 4):
        mine = mine + pltpu.roll(mine, HALF - reach, 1)
    held[...] = mine
    copy = pltpu.make_async_copy(held, wanted, sem)
    copy.start()

    left_low[...] = low_in[...]
    left_high[...] = high_in[...]
    messages = (m0, m1, m2, m3)
    given = [(link[...] * message[0:SIDE, :],) for link, message in zip((l0, l1, l2, l3), messages)]

    def apply(rows, lanes, more):
        if lanes != LANES[1]:
            left_low[rows, :] += more[0][:, 0:HALF]
        if lanes != LANES[0]:
            left_high[rows, :] += more[0][:, more[0].shape[1] - HALF :]

    from_peers(table, given, apply)
    write_coarse(restricted(left_low, left_high), coarse_left, 0)
    copy.wait()
    for target in range(send_ref.shape[0]):
        chosen = jnp.maximum(wanted[0, target * COARSE_DEV] - 1, 0)
        send_ref[target, 0:SIDE, :] = coarse_left[chosen]
        send_ref[target, SIDE : 3 * SIDE, :] = coarse_coefs[chosen]


def restricted(*parts):
    rows = BRK * SIDE // 2
    paired = jnp.concatenate(
        [part[pl.ds(0, rows, stride=2), :] + part[pl.ds(1, rows, stride=2), :] for part in parts], axis=1
    )
    fine = lax.broadcasted_iota(I32, (PLANE, HALF), 0)
    target = lax.broadcasted_iota(I32, (PLANE, HALF), 1)
    same = (fine // (2 * SIDE) == target // SIDE) & ((fine % SIDE) // 2 == target % SIDE)
    table = jnp.where(same, 0.125, 0.0).astype(jnp.bfloat16)
    total = jnp.zeros((rows, HALF), F32)
    rest = paired
    for _ in range(3):
        part = rest.astype(jnp.bfloat16)
        total = total + jnp.dot(part, table, preferred_element_type=F32)
        rest = rest - part.astype(F32)
    return total


def coarse_tiles(values):
    depth = SIDE // 2
    for coarse in range(COARSE_DEV):
        cz, cy, cx = coarse // 4, coarse // 2 % 2, coarse % 2
        for pz in range(2):
            for py in range(2):
                fine = ((2 * cz + pz) * EDGE + 2 * cy + py) * EDGE + 2 * cx
                left = values[fine * depth : (fine + 1) * depth, :]
                right = values[(fine + 1) * depth : (fine + 2) * depth, :]
                yield coarse, pz, py, left + pltpu.roll(right, depth, 1)


def write_coarse(values, out_ref, base):
    for coarse, pz, py, tile in coarse_tiles(values):
        top = base + pz * (SIDE // 2)
        out_ref[coarse, top : top + SIDE // 2, py * HALF : (py + 1) * HALF] = tile


def coefficient_kernel(kappa_ref, decay_ref, out_ref, low, high):
    for ref, base in ((kappa_ref, 0), (decay_ref, SIDE)):
        low[...] = ref[0 : BRK * SIDE, 0:HALF]
        high[...] = ref[0 : BRK * SIDE, HALF:PLANE]
        write_coarse(restricted(low, high), out_ref, base)


def place_kernel(per_row, coarse_source, arrived, out_ref, sem):
    copies = [
        pltpu.make_async_copy(arrived.at[coarse_source[slot] // per_row], out_ref.at[slot], sem.at[slot])
        for slot in range(COARSE_DEV)
    ]
    for copy in copies:
        copy.start()
    for copy in copies:
        copy.wait()


def paired(block, axis, offset):
    size = lax.axis_size(axis)
    route = []
    for first in range(offset, size + offset, 2):
        one, two = first % size, (first + 1) % size
        route += [(one, two), (two, one)]
    return lax.ppermute(block, axis, route)


def shifted(block, axis, distance):
    size = lax.axis_size(axis)
    return lax.ppermute(block, axis, [(place, (place + distance) % size) for place in range(size)])


def exchanged(outgoing):
    return [
        paired(outgoing[0], "brick", 0),
        paired(outgoing[1], "brick", 1),
        paired(outgoing[2], "sub", 0),
        paired(outgoing[3], "sub", 1),
    ]


VMEM_SPEC = pl.BlockSpec(memory_space=pltpu.VMEM)
SMEM_SPEC = pl.BlockSpec(memory_space=pltpu.SMEM)
HBM_SPEC = pl.BlockSpec(memory_space=pltpu.HBM)


def in_hbm(array):
    return pltpu.with_memory_space_constraint(array, pltpu.HBM)


def in_vmem(*shape):
    return pltpu.VMEM(shape, F32)


def kernel_call(kernel, name, ins, outs, out_specs=None, scratch=()):
    return pl.pallas_call(
        kernel,
        out_shape=outs,
        in_specs=ins,
        out_specs=out_specs if out_specs is not None else tuple(VMEM_SPEC for _ in outs),
        scratch_shapes=list(scratch),
        compiler_params=pltpu.CompilerParams(vmem_limit_bytes=VMEM_LIMIT),
        name=name,
    )


def body(field_start, source, diffusion, decay_rate, neighbour, coarse_source):
    subs = lax.axis_size("sub")
    rows = BRK * SIDE
    field_start, source, diffusion, decay_rate = (
        array.reshape(rows, PLANE) for array in (field_start, source, diffusion, decay_rate)
    )
    known_shape = in_vmem(KNOWN_ROWS, HALF)
    whole = in_vmem(rows, PLANE)
    extended = in_vmem(EXT_BRICKS * SIDE, PLANE)
    message = (in_vmem(SIDE + KNOWN_ROWS, PLANE),) * 2 + (in_vmem(SIDE, PLANE),) * 2
    double = (in_vmem(2 * SIDE + KNOWN_ROWS, PLANE),) * 2 + (in_vmem(2 * SIDE, PLANE),) * 2

    table, field_start, diffusion, *outgoing, known = kernel_call(
        functools.partial(start_kernel, subs),
        "route_and_pack",
        [HBM_SPEC] * 4,
        (jax.ShapeDtypeStruct((8, 128), I32),) + (extended,) * 2 + double + (known_shape,),
        out_specs=(SMEM_SPEC,) + (VMEM_SPEC,) * 7,
        scratch=[
            pltpu.VMEM((2, HALF), I32),
            pltpu.VMEM((SEND_ROW, HALF), I32),
            pltpu.SMEM((COARSE_DEV,), I32),
            pltpu.VMEM((6, BRK), I32),
            pltpu.SemaphoreType.DMA(()),
            pltpu.SemaphoreType.DMA(()),
            pltpu.SemaphoreType.DMA(()),
            pltpu.SemaphoreType.DMA(()),
            pltpu.SemaphoreType.DMA((2 * CHUNKS,)),
        ],
    )(*(in_hbm(array) for array in (coarse_source, neighbour.T, field_start, diffusion)))
    own_faces = outgoing
    incoming = exchanged(outgoing)
    bricks_along = lax.axis_size("brick")
    other = shifted(known, "brick", bricks_along // 4)

    coefs, diagonal, total, source, decay_rate = kernel_call(
        links_kernel,
        "links",
        [SMEM_SPEC] + [VMEM_SPEC] * 2 + [HBM_SPEC] * 2,
        (in_vmem(6, rows, PLANE),) + (whole,) * 4,
        scratch=[pltpu.SemaphoreType.DMA((2 * CHUNKS,))],
    )(table, field_start, diffusion, in_hbm(source), in_hbm(decay_rate))
    coarse_coefs = kernel_call(
        coefficient_kernel, "coarse_coefficients", [VMEM_SPEC] * 2, (in_vmem(COARSE_DEV, 2 * SIDE, PLANE),),
        scratch=[pltpu.VMEM((rows, HALF), F32), pltpu.VMEM((rows, HALF), F32)],
    )(diffusion, decay_rate)[0]
    diagonal, field, scale, known, *rest = kernel_call(
        first_kernel,
        "first_sweep",
        [SMEM_SPEC] + [VMEM_SPEC] * 15,
        (whole, extended, whole, known_shape) + (in_vmem(SIDE, PLANE),) * PEERS + message,
    )(table, diagonal, total, source, decay_rate, field_start, known, other, *own_faces, *incoming)
    far_links, outgoing = rest[:PEERS], rest[PEERS:]
    incoming = exchanged(outgoing)
    other = shifted(known, "brick", bricks_along // 2)
    for _ in range(SWEEPS - 1):
        field = kernel_call(
            sweep_kernel,
            "next_sweep",
            [SMEM_SPEC] + [VMEM_SPEC] * 4,
            (whole,),
        )(table, field, source, coefs, scale)[0]
        field, known, *outgoing = kernel_call(
            sweep_rest_kernel,
            "next_sweep_rest",
            [SMEM_SPEC] + [VMEM_SPEC] * 12,
            (extended, known_shape) + message,
        )(table, field, scale, known, other, *far_links, *incoming)
        incoming = exchanged(outgoing)
    left = in_vmem(rows, HALF)
    left_low, left_high, field = kernel_call(
        residual_kernel,
        "residual",
        [SMEM_SPEC] + [VMEM_SPEC] * 4,
        (left, left, jax.ShapeDtypeStruct((rows, PLANE), F32)),
        out_specs=(VMEM_SPEC, VMEM_SPEC, HBM_SPEC),
        scratch=[pltpu.SemaphoreType.DMA(())],
    )(table, field, source, coefs, diagonal)
    send = kernel_call(
        functools.partial(residual_rest_kernel, subs),
        "residual_rest",
        [SMEM_SPEC] + [VMEM_SPEC] * 12,
        (in_vmem(bricks_along, 3 * SIDE, PLANE),),
        scratch=[
            pltpu.VMEM((rows, HALF), F32),
            pltpu.VMEM((rows, HALF), F32),
            pltpu.VMEM((COARSE_DEV, SIDE, PLANE), F32),
            pltpu.VMEM((KNOWN_ROWS, HALF), I32),
            pltpu.SMEM((KNOWN_ROWS, HALF), I32),
            pltpu.SemaphoreType.DMA(()),
        ],
    )(table, left_low, left_high, known, coarse_coefs, *far_links, *incoming)[0]
    arrived = lax.all_to_all(send, "brick", split_axis=0, concat_axis=0, tiled=True)
    moved = kernel_call(
        functools.partial(place_kernel, subs * COARSE_DEV),
        "place",
        [SMEM_SPEC, HBM_SPEC],
        jax.ShapeDtypeStruct((COARSE_DEV, 3 * SIDE, PLANE), F32),
        out_specs=HBM_SPEC,
        scratch=[pltpu.SemaphoreType.DMA((COARSE_DEV,))],
    )(coarse_source, arrived)
    return field.reshape(BRK, SIDE, PLANE), moved.reshape(COARSE_DEV, 3, SIDE, PLANE)


def solution(mesh):
    placed = (
        P(("brick", "sub"), None, None),
        P(("brick", "sub"), None, None),
        P(("brick", "sub"), None, None),
        P(("brick", "sub"), None, None),
        P(("brick", "sub"), None),
        P(("brick", "sub")),
    )
    return jax.shard_map(
        body,
        mesh=mesh,
        in_specs=placed,
        out_specs=(P(("brick", "sub"), None, None), P(("brick", "sub"), None, None, None)),
        check_vma=False,
    )
```
